128 devices in a mesh: dom: 8 (over z, core), ml: 16 (over x, y).
Axes of the slice: x: 4, y: 4, z: 4, core: 2. Of those that a mesh axis runs over, the one named last changes fastest.
Arguments:
- mm_positions: float32 [3, 262144], P(None, ('dom', 'ml')), may hold values from -6 to 6
- mm_charge: float32 [262144], P(('dom', 'ml')), may hold values from -1 to 1
- mm_tiles: int32 [2048, 8], P(('dom', 'ml')), may hold values from 0 to 47, as said below
- ml_feat: bfloat16 [64, 512, 128], P('dom', 'ml'), may hold values from -6 to 6
- ml_positions: float32 [64, 3, 512], P('dom', None, 'ml'), may hold values from -6 to 6
- ml_neighbours: int32 [64, 32, 512], P('dom', None, 'ml'), may hold values from 0 to 511
- msg_weight: bfloat16 [2, 128, 128], replicated, may hold values from -0.5 to 0.5
- radial_weight: float32 [2, 8, 128], replicated, may hold values from -5 to 5
- out_weight: bfloat16 [2, 128, 128], replicated, may hold values from -0.5 to 0.5
- read_weight: bfloat16 [128, 256], replicated, may hold values from -0.5 to 0.5
Outputs:
- mm_force: float32 [3, 262144], P(None, ('dom', 'ml'))
- ml_force: float32 [64, 3, 512], P('dom', None, 'ml')
The draws below stay inside these ranges and needn't reach their ends.
Inputs may be any that keep to these rules, and one draw needn't show every extreme that they name: `mm_tiles`: for each tile of a device, 8 distinct positions among the 16 tiles of the previous device along dom+ml (wrapping), its own tiles and the next device's, in that order; at least one lies among the previous device's tiles and at least one among the next device's. `ml_neighbours`: indices of atoms within the same patch.
All inputs are finite; a program needn't handle non-finite values.
Results may differ from the reference program's by a relative error of at most 0.007.
Values may be sent and summed in bfloat16 or wider, within the bound.
No kernel may reach another device: no remote copies, remote signals or barrier semaphores. Data moves between devices by JAX's collectives and lax.ppermute only.
A program may use at most 320 MiB of HBM per device.

```python
import math
import jax
import jax.numpy as jnp
from jax import lax

F = 128
LAYERS = 2
NB = 8
K = 32
P_SIZE = 512
TILE = 128
TILES_DEV = 16
NEIGHBOR_TILES = 8
NP = 64
NTILE = 2048
NMM = 262144


def draw_mm_tiles(key, part):
    key = jax.random.fold_in(key, 11)
    window = 3 * TILES_DEV
    score_key, low_key, high_key = jax.random.split(key, 3)
    ranking_values = jax.random.randint(score_key, (NTILE, window), 0, 1 << 20)
    ranking_values = ranking_values * window + jnp.arange(window, dtype=jnp.int32)[None, :]
    lower_selection = jax.random.randint(low_key, (NTILE, 1), 0, TILES_DEV)
    upper_selection = jax.random.randint(high_key, (NTILE, 1), 2 * TILES_DEV, 3 * TILES_DEV)
    column_slots = jnp.arange(window, dtype=jnp.int32)[None, :]
    extra_reward = jnp.where(column_slots == lower_selection, 1 << 28, 0) + jnp.where(column_slots == upper_selection, 1 << 28, 0)
    selected_entries = lax.top_k(ranking_values + extra_reward, NEIGHBOR_TILES)[1]
    return selected_entries.astype(jnp.int32)


def place_ends(values, own_key, least, high):
    index_at = [jax.random.randint(jax.random.fold_in(own_key, axis), (), 0, length) for axis, length in enumerate(values.shape)]
    longest = values.shape.index(max(values.shape))
    beside = index_at[:longest] + [(index_at[longest] + 1) % values.shape[longest]] + index_at[longest + 1:]
    return values.at[tuple(index_at)].set(least).at[tuple(beside)].set(high)


def level_of(own_key, dims, cuts, least, largest):
    factor_of = 1.0
    for position, parts in cuts:
        draws = jax.random.uniform(jax.random.fold_in(jax.random.fold_in(own_key, 6), position), (parts,), jnp.float32, least / len(cuts), largest / len(cuts))
        factor_of = factor_of * jnp.repeat(jnp.exp(draws), dims[position] // parts).reshape((-1,) + (1,) * (len(dims) - 1 - position))
    return factor_of


def scatter_about(rng, shape, spread, most, cuts=(), kind=jnp.bfloat16):
    values = jax.random.normal(rng, shape, jnp.float32) * spread
    if len(cuts) > 0:
        values = level_of(rng, shape, cuts, -0.22, 0.18) * values
    return jnp.clip(values, min=-most, max=most).astype(kind)


def setup_inputs(seed: int = 0) -> dict:
    arg_keys = jax.random.split(jax.random.key(seed), 11)
    mm_positions = scatter_about(arg_keys[0], (3, NMM), 1.0, 6.0, ((1, 128),), jnp.float32)
    mm_charge = jnp.clip(jax.random.uniform(arg_keys[1], (NMM,), jnp.float32, -1.0, 1.0) * level_of(arg_keys[1], (NMM,), ((0, 128),), -0.4, 0.0), -1.0, 1.0)
    mm_tiles = draw_mm_tiles(jax.random.fold_in(arg_keys[10], 71), 0)
    ml_feat = scatter_about(arg_keys[3], (NP, P_SIZE, F), 1.0, 6.0, ((0, 8), (1, 16)))
    ml_positions = scatter_about(arg_keys[4], (NP, 3, P_SIZE), 1.5, 6.0, ((0, 8), (2, 16)), jnp.float32)
    ml_neighbours = place_ends(jax.random.randint(arg_keys[5], (NP, K, P_SIZE), 0, P_SIZE), jax.random.fold_in(arg_keys[5], 1), 0, P_SIZE - 1).astype(jnp.int32)
    msg_weight = scatter_about(arg_keys[6], (LAYERS, F, F), F ** -0.5, 0.5)
    radial_weight = scatter_about(arg_keys[7], (LAYERS, NB, F), 1.0, 5.0, (), jnp.float32)
    out_weight = scatter_about(arg_keys[8], (LAYERS, F, F), F ** -0.5, 0.5)
    read_weight = scatter_about(arg_keys[9], (F, 2 * F), F ** -0.5, 0.5)
    return dict(mm_positions=mm_positions, mm_charge=mm_charge, mm_tiles=mm_tiles, ml_feat=ml_feat, ml_positions=ml_positions, ml_neighbours=ml_neighbours, msg_weight=msg_weight, radial_weight=radial_weight, out_weight=out_weight, read_weight=read_weight)


RADIUS = 6.0
SOFTEN = 1.0
COULOMB = 0.5

def pair_force(own_tile, near_tiles):
    offsets = own_tile[:3, None, :, None] - near_tiles[:3, :, None, :]
    squared = lax.optimization_barrier(jnp.sum(offsets * offsets, axis=0)) + SOFTEN
    inverse = 1.0 / (squared * jnp.sqrt(squared))
    strength = COULOMB * own_tile[3][None, :, None] * near_tiles[3][:, None, :] * inverse
    return lax.optimization_barrier(jnp.sum(strength[None] * offsets, axis=(1, 3)))

def patch_model(pieces, msg_weight, radial_weight, out_weight, read_weight):
    features, positions, neighbours = pieces
    offsets = positions[:, neighbours] - positions[:, None, :]
    distance = jnp.sqrt(lax.optimization_barrier(jnp.sum(offsets * offsets, axis=0)) + 1.0)
    envelope = 0.5 * (jnp.cos(jnp.pi * jnp.minimum(distance / RADIUS, 1.0)) + 1.0)
    centers = jnp.arange(NB).astype(jnp.float32) * (RADIUS / NB)
    radial_basis = jnp.exp(-2.0 * (distance[None] - centers[:, None, None]) ** 2) * envelope[None]
    norm_factor = 1.0 / math.sqrt(K)
    hidden = features
    for layer_index in range(LAYERS):
        mixed_feat = jnp.dot(hidden, msg_weight[layer_index], preferred_element_type=jnp.float32).astype(jnp.bfloat16)
        radial = jnp.einsum('nkp,nc->kpc', radial_basis, radial_weight[layer_index].astype(jnp.float32), precision=lax.Precision.HIGHEST)
        message = lax.optimization_barrier(jnp.sum(radial * mixed_feat[neighbours].astype(jnp.float32), axis=0)) * norm_factor
        active = jax.nn.silu(message).astype(jnp.bfloat16)
        update = jnp.dot(active, out_weight[layer_index], preferred_element_type=jnp.float32)
        hidden = (hidden.astype(jnp.float32) + update).astype(jnp.bfloat16)
    readout = jnp.dot(hidden, read_weight, preferred_element_type=jnp.float32).astype(jnp.bfloat16)
    query_feat = readout[:, :F].astype(jnp.float32)
    key_feat = readout[:, F:].astype(jnp.float32)
    strength = jnp.einsum('pc,kpc->kp', query_feat, key_feat[neighbours]) / F * envelope
    return lax.optimization_barrier(jnp.sum(strength[None] * offsets, axis=1))

def reference(mm_positions, mm_charge, mm_tiles, ml_feat, ml_positions, ml_neighbours, msg_weight, radial_weight, out_weight, read_weight):
    mm_atoms = jnp.concatenate([mm_positions, mm_charge[None]], axis=0).reshape(4, NTILE, TILE)

    def tile_force(tile_index):
        slab_index = tile_index // TILES_DEV
        global_tile = (slab_index * TILES_DEV - TILES_DEV + mm_tiles[tile_index]) % NTILE
        return pair_force(mm_atoms[:, tile_index], mm_atoms[:, global_tile])
    tile_forces = lax.map(tile_force, jnp.arange(NTILE).astype(jnp.int32))
    mm_force = tile_forces.transpose(1, 0, 2).reshape(3, NMM)

    def run_patch(pieces):
        return patch_model(pieces, msg_weight, radial_weight, out_weight, read_weight)
    ml_force = lax.map(run_patch, (ml_feat, ml_positions, ml_neighbours))
    return (mm_force, ml_force)
```

```python
import math

import jax
import jax.numpy as jnp
from jax import lax
from jax.experimental import pallas as pl
from jax.experimental.pallas import tpu as pltpu
from jax.sharding import PartitionSpec as P

TILE = 128
RADIUS = 6.0
SOFTEN = 1.0
COULOMB = 0.5
HALVES = 2

COSINE = (
    0.9999999991255941,
    -0.23370050635000697,
    0.019968606683524803,
    -0.0008935362638784474,
    2.3601070666008123e-05,
)

F32 = jnp.float32
BF16 = jnp.bfloat16


def pack_kernel(feat_ref, pos_ref, nb_ref, mm_pos_ref, mm_charge_ref, send_ref, atoms_ref, geo_ref):
    patches, atoms, _ = feat_ref.shape
    geo_ref[...] = jnp.zeros_like(geo_ref)
    for p in range(patches):
        numbers = (nb_ref[p] - 256).astype(F32)
        geo_ref[p, 0:16, 0:32] = numbers[0:16]
        geo_ref[p, 0:16, 32:64] = numbers[16:32]
        place = pos_ref[p]
        high = place.astype(BF16).astype(F32)
        rest = place - high
        middle = rest.astype(BF16).astype(F32)
        geo_ref[p, 0:3, 64:96] = high
        geo_ref[p, 0:3, 96:128] = middle
        geo_ref[p, 8:11, 64:96] = rest - middle
        block = geo_ref[p].astype(BF16)
        for half in range(HALVES):
            send_ref[half * patches + p, 0:atoms, :] = feat_ref[p]
            send_ref[half * patches + p, atoms : atoms + 16, :] = block
    atoms_ref[0:3, :] = mm_pos_ref[...]
    atoms_ref[3:4, :] = mm_charge_ref[...]


def patch_kernel(
    half_ref,
    recv_ref,
    msg_ref,
    radial_ref,
    out_w_ref,
    read_ref,
    force_ref,
    hidden_ref,
    pos_ref,
    place_ref,
    low_ref,
    unit_ref,
    count_ref,
    basis_ref,
    pull_ref,
    next_ref,
):
    sources = recv_ref.shape[0]
    share = recv_ref.shape[1] - 16
    size = sources * share
    own = size // HALVES
    neighbours = low_ref.shape[0]
    basis_count = radial_ref.shape[1]
    layers = msg_ref.shape[0]
    channels = recv_ref.shape[2]

    for m in range(sources):
        hidden_ref[share * m : share * (m + 1), :] = recv_ref[m, 0:share, :]
        geo = recv_ref[m, share : share + 16, :].astype(F32)
        lanes = slice(share * m, share * (m + 1))
        pos_ref[:, lanes] = (geo[0:8, 64:96] + geo[0:8, 96:128]) + geo[8:16, 64:96]
        low_ref[0:16, lanes] = geo[:, 0:32].astype(jnp.int32) + 256
        low_ref[16:32, lanes] = geo[:, 32:64].astype(jnp.int32) + 256
    place_ref[...] = jnp.transpose(pos_ref[...])
    index = low_ref[...]
    low_ref[...] = index & 127
    unit_ref[...] = jnp.int32(1) << ((index >> 7) << 3)

    rows = lax.broadcasted_iota(jnp.int32, (128, 128), 0)
    for block in range(size // 128):
        lanes = slice(128 * block, 128 * (block + 1))
        total = jnp.zeros((128, 128), jnp.int32)
        for k in range(neighbours):
            total += jnp.where(rows == low_ref[k : k + 1, lanes], unit_ref[k : k + 1, lanes], 0)
        count_ref[lanes, :] = jnp.transpose(total)

    step = 16

    def pairs(block, carry):
        own_rows = pl.ds(pl.multiple_of(block * step, step), step)
        squared = SOFTEN
        for axis in range(3):
            offset = pos_ref[axis : axis + 1, :] - place_ref[own_rows, axis : axis + 1]
            squared = offset * offset + squared
        packed = count_ref[own_rows, :]
        times = jnp.concatenate(
            [(packed >> (8 * f)) & 255 for f in range(size // 128)], axis=1
        ).astype(F32)
        near = jnp.minimum(squared, RADIUS * RADIUS)
        u = near * (1.0 / (RADIUS * RADIUS))
        series = COSINE[4]
        for value in COSINE[3::-1]:
            series = series * u + value
        root = (1.0 - u) * series
        envelope = root * root * times
        pull_ref[own_rows, :] = envelope
        distance = near * lax.rsqrt(near)
        growth = jnp.exp(distance * (4.0 * RADIUS / basis_count))
        basis = jnp.exp(near * -2.0) * envelope
        for n in range(basis_count):
            basis_ref[n, own_rows, :] = basis.astype(BF16)
            if n + 1 < basis_count:
                basis = basis * growth
        return carry

    lax.fori_loop(0, size // step, pairs, 0)

    number = lax.broadcasted_iota(jnp.int32, (basis_count, channels), 0).astype(F32)
    center = number * (RADIUS / basis_count)
    scale = jnp.exp(center * center * -2.0) * (1.0 / math.sqrt(neighbours))
    chunk = 256
    for layer in range(layers):
        mixed = jnp.dot(
            hidden_ref[...], msg_ref[layer], preferred_element_type=F32
        ).astype(BF16)
        radial = radial_ref[layer] * scale
        for block in range(size // chunk):
            part = slice(chunk * block, chunk * (block + 1))
            message = jnp.zeros((chunk, channels), F32)
            for n in range(basis_count):
                message += radial[n : n + 1, :] * jnp.dot(
                    basis_ref[n, part, :], mixed, preferred_element_type=F32
                )
            active = jax.nn.silu(message).astype(BF16)
            update = jnp.dot(active, out_w_ref[layer], preferred_element_type=F32)
            next_ref[part, :] = (hidden_ref[part, :].astype(F32) + update).astype(BF16)
        hidden_ref[...] = next_ref[...]

    start = pl.multiple_of(half_ref[0] * own, own)
    key = jnp.dot(
        hidden_ref[...], read_ref[:, channels:], preferred_element_type=F32
    ).astype(BF16)
    query = jnp.dot(
        hidden_ref[pl.ds(start, own), :], read_ref[:, :channels], preferred_element_type=F32
    ).astype(BF16)
    lane = lax.broadcasted_iota(jnp.int32, (64, 128), 1)
    force_ref[...] = jnp.zeros_like(force_ref)
    for part in range(own // 128):
        columns = []
        for piece in range(2):
            first = 128 * part + 64 * piece
            here = pl.ds(start + first, 64)
            pull = lax.dot_general(
                query[first : first + 64],
                key,
                (((1,), (1,)), ((), ())),
                preferred_element_type=F32,
            ) * (pull_ref[here, :] * (1.0 / channels))
            column = jnp.zeros((64, 128), F32)
            for axis in range(3):
                offset = pos_ref[axis : axis + 1, :] - place_ref[here, axis : axis + 1]
                total = jnp.sum(pull * offset, axis=1, keepdims=True)
                column = jnp.where(lane == axis, total, column)
            columns.append(column)
        turned = jnp.transpose(jnp.concatenate(columns, axis=0))[0:8]
        for a in range(128 // share):
            force_ref[128 // share * part + a, :, 0:share] = turned[:, share * a : share * (a + 1)]


def pair_kernel(tiles_ref, own_ref, low_ref, high_ref, force_ref, window_ref, place_ref):
    tiles, listed = tiles_ref.shape
    for which, ref in enumerate((low_ref, own_ref, high_ref)):
        for t in range(tiles):
            window_ref[which * tiles + t, 0:4, :] = ref[:, TILE * t : TILE * (t + 1)]
    for t in range(tiles):
        place_ref[TILE * t : TILE * (t + 1), 0:4] = jnp.transpose(
            own_ref[:, TILE * t : TILE * (t + 1)]
        )
    group = 32
    lane = lax.broadcasted_iota(jnp.int32, (group, 128), 1)

    def one_tile(t, carry):
        near = [tiles_ref[t, c] for c in range(listed)]
        columns = []
        for part in range(TILE // group):
            here = pl.ds(pl.multiple_of(t * TILE + part * group, group), group)
            mine = [place_ref[here, axis : axis + 1] for axis in range(4)]
            sums = [jnp.zeros((group, 128), F32) for _ in range(3)]
            for c in range(listed):
                offsets = [mine[axis] - window_ref[near[c], axis : axis + 1, :] for axis in range(3)]
                squared = SOFTEN
                for offset in offsets:
                    squared = offset * offset + squared
                inverse = lax.rsqrt(squared)
                strength = window_ref[near[c], 3:4, :] * inverse * (inverse * inverse)
                sums = [total + strength * offset for total, offset in zip(sums, offsets)]
            column = jnp.zeros((group, 128), F32)
            for axis in range(3):
                total = jnp.sum(sums[axis], axis=1, keepdims=True) * (COULOMB * mine[3])
                column = jnp.where(lane == axis, total, column)
            columns.append(column)
        turned = jnp.transpose(jnp.concatenate(columns, axis=0))
        force_ref[:, pl.ds(pl.multiple_of(t * TILE, TILE), TILE)] = turned[0:3]
        return carry

    lax.fori_loop(0, tiles, one_tile, 0)


def vmem(count):
    return [pl.BlockSpec(memory_space=pltpu.VMEM)] * count


def on_device(
    mm_positions,
    mm_charge,
    mm_tiles,
    ml_feat,
    ml_positions,
    ml_neighbours,
    msg_weight,
    radial_weight,
    out_weight,
    read_weight,
):
    patches, share, channels = ml_feat.shape
    atom_count = mm_positions.shape[1]
    tile_count, listed = mm_tiles.shape
    members = lax.axis_size("ml")
    size = members * share
    own = size // HALVES
    neighbours = ml_neighbours.shape[1]
    basis_count = radial_weight.shape[1]
    limit = 48 * 1024 * 1024

    send, atoms = pl.pallas_call(
        pack_kernel,
        out_shape=(
            jax.ShapeDtypeStruct((members, share + 16, channels), BF16),
            jax.ShapeDtypeStruct((4, atom_count), F32),
        ),
        in_specs=vmem(5),
        out_specs=tuple(vmem(2)),
        scratch_shapes=[pltpu.VMEM((patches, 16, 128), F32)],
        cost_estimate=pl.CostEstimate(flops=1000, bytes_accessed=400000, transcendentals=0),
    )(ml_feat, ml_positions, ml_neighbours, mm_positions, mm_charge.reshape(1, atom_count))
    recv = lax.all_to_all(send, "ml", split_axis=0, concat_axis=0, tiled=True)

    devices = lax.axis_size(("dom", "ml"))
    forward = [(i, (i + 1) % devices) for i in range(devices)]
    backward = [(b, a) for a, b in forward]
    low = lax.ppermute(atoms, ("dom", "ml"), forward)
    high = lax.ppermute(atoms, ("dom", "ml"), backward)

    half = (lax.axis_index("ml") // patches).astype(jnp.int32).reshape(1)
    forces = pl.pallas_call(
        patch_kernel,
        out_shape=jax.ShapeDtypeStruct((own // share, 8, 128), F32),
        in_specs=[pl.BlockSpec(memory_space=pltpu.SMEM)] + vmem(5),
        out_specs=vmem(1)[0],
        scratch_shapes=[
            pltpu.VMEM((size, channels), BF16),
            pltpu.VMEM((8, size), F32),
            pltpu.VMEM((size, 8), F32),
            pltpu.VMEM((neighbours, size), jnp.int32),
            pltpu.VMEM((neighbours, size), jnp.int32),
            pltpu.VMEM((size, 128), jnp.int32),
            pltpu.VMEM((basis_count, size, size), BF16),
            pltpu.VMEM((size, size), F32),
            pltpu.VMEM((size, channels), BF16),
        ],
        compiler_params=pltpu.CompilerParams(vmem_limit_bytes=limit),
        cost_estimate=pl.CostEstimate(
            flops=5 * 10**9, bytes_accessed=1000000, transcendentals=10**6
        ),
    )(half, recv, msg_weight, radial_weight, out_weight, read_weight)
    groups = [[h * patches + p for p in range(patches)] for h in range(HALVES)]
    returned = lax.all_to_all(
        forces, "ml", split_axis=0, concat_axis=0, tiled=True, axis_index_groups=groups
    )
    ml_force = returned[:, :3, :share]

    mm_force = pl.pallas_call(
        pair_kernel,
        out_shape=jax.ShapeDtypeStruct((3, atom_count), F32),
        in_specs=[pl.BlockSpec(memory_space=pltpu.SMEM)] + vmem(3),
        out_specs=vmem(1)[0],
        scratch_shapes=[
            pltpu.VMEM((3 * tile_count, 8, TILE), F32),
            pltpu.VMEM((atom_count, 8), F32),
        ],
        compiler_params=pltpu.CompilerParams(vmem_limit_bytes=limit),
        cost_estimate=pl.CostEstimate(
            flops=4 * 10**9, bytes_accessed=200000, transcendentals=10**6
        ),
    )(mm_tiles, atoms, low, high)
    return (mm_force, ml_force)


def solution(mesh):
    in_specs = (
        P(None, ("dom", "ml")),
        P(("dom", "ml")),
        P(("dom", "ml"), None),
        P("dom", "ml", None),
        P("dom", None, "ml"),
        P("dom", None, "ml"),
        P(),
        P(),
        P(),
        P(),
    )
    out_specs = (P(None, ("dom", "ml")), P("dom", None, "ml"))
    return jax.shard_map(
        on_device, mesh=mesh, in_specs=in_specs, out_specs=out_specs, check_vma=False
    )
```

```python
import math

import jax
import jax.numpy as jnp
from jax import lax
from jax.experimental import pallas as pl
from jax.experimental.pallas import tpu as pltpu
from jax.sharding import PartitionSpec as P

TILE = 128
RADIUS = 6.0
SOFTEN = 1.0
COULOMB = 0.5
HALVES = 2

COSINE = (
    0.9999999991255941,
    -0.23370050635000697,
    0.019968606683524803,
    -0.0008935362638784474,
    2.3601070666008123e-05,
)

F32 = jnp.float32
BF16 = jnp.bfloat16


def split(value):
    high = value.astype(BF16).astype(F32)
    rest = value - high
    middle = rest.astype(BF16).astype(F32)
    return high, middle, rest - middle


LEFT = (0, 0, 1, 1, 0, 2)
RIGHT = (0, 1, 0, 1, 2, 0)


def left_rows(rows_ref, pieces, norm):
    for g, which in enumerate(LEFT):
        rows_ref[4 * g : 4 * g + 4, :] = pieces[which]
    for g, value in enumerate(split(norm + SOFTEN)):
        rows_ref[24 + g : 25 + g, :] = value
    rows_ref[27:30, :] = jnp.ones((3, norm.shape[1]), F32)
    rows_ref[30:32, :] = jnp.zeros((2, norm.shape[1]), F32)


def right_rows(rows_ref, pieces, norm):
    for g, which in enumerate(RIGHT):
        rows_ref[4 * g : 4 * g + 4, :] = pieces[which] * -2.0
    rows_ref[24:27, :] = jnp.ones((3, norm.shape[1]), F32)
    for g, value in enumerate(split(norm)):
        rows_ref[27 + g : 28 + g, :] = value
    rows_ref[30:32, :] = jnp.zeros((2, norm.shape[1]), F32)


def norm_of(place):
    return place[0:1] * place[0:1] + place[1:2] * place[1:2] + place[2:3] * place[2:3]


def pack_kernel(feat_ref, pos_ref, nb_ref, mm_pos_ref, mm_charge_ref, send_ref, atoms_ref, geo_ref):
    patches, atoms, _ = feat_ref.shape
    geo_ref[...] = jnp.zeros_like(geo_ref)
    high, middle, low = split(pos_ref[...])
    for p in range(patches):
        numbers = (nb_ref[p] - 256).astype(F32)
        geo_ref[p, 0:16, 0:32] = numbers[0:16]
        geo_ref[p, 0:16, 32:64] = numbers[16:32]
        for axis in range(3):
            geo_ref[p, axis : axis + 1, 64:96] = high[axis, p : p + 1]
            geo_ref[p, axis : axis + 1, 96:128] = middle[axis, p : p + 1]
            geo_ref[p, axis + 8 : axis + 9, 64:96] = low[axis, p : p + 1]
        block = geo_ref[p].astype(BF16)
        for half in range(HALVES):
            send_ref[half * patches + p, 0:atoms, :] = feat_ref[p]
            send_ref[half * patches + p, atoms : atoms + 16, :] = block
    atoms_ref[0:3, :] = mm_pos_ref[...]
    atoms_ref[3:4, :] = mm_charge_ref[...]


def patch_kernel(
    half_ref,
    recv_ref,
    msg_ref,
    radial_ref,
    out_w_ref,
    read_ref,
    force_ref,
    hidden_ref,
    pos_ref,
    rows_ref,
    near_ref,
    mine_ref,
    side_ref,
    low_ref,
    unit_ref,
    count_ref,
    square_ref,
    basis_ref,
    pull_ref,
    active_ref,
):
    sources = recv_ref.shape[0]
    share = recv_ref.shape[1] - 16
    size = sources * share
    own = size // HALVES
    neighbours = low_ref.shape[0]
    basis_count = radial_ref.shape[1]
    layers = msg_ref.shape[0]
    channels = recv_ref.shape[2]
    blocks = basis_ref.shape[0]
    height = size // blocks
    tiles = size // 128

    for m in range(sources):
        hidden_ref[share * m : share * (m + 1), :] = recv_ref[m, 0:share, :]
        geo = recv_ref[m, share : share + 16, :].astype(F32)
        lanes = slice(share * m, share * (m + 1))
        pos_ref[:, lanes] = (geo[0:8, 64:96] + geo[0:8, 96:128]) + geo[8:16, 64:96]
        low_ref[0:16, lanes] = geo[:, 0:32].astype(jnp.int32) + 256
        low_ref[16:32, lanes] = geo[:, 32:64].astype(jnp.int32) + 256

    def mix(layer):
        return jnp.dot(hidden_ref[...], msg_ref[layer], preferred_element_type=F32).astype(BF16)

    mixed = mix(0)

    place = pos_ref[0:4, :]
    pieces = split(place)
    norm = norm_of(place)
    right_rows(rows_ref, pieces, norm)
    near_ref[...] = rows_ref[...].astype(BF16)
    left_rows(rows_ref, pieces, norm)
    for b in range(tiles):
        at = slice(128 * b, 128 * (b + 1))
        mine_ref[at, :] = jnp.transpose(rows_ref[:, at]).astype(BF16)
    for g, value in enumerate(pieces):
        rows_ref[4 * g : 4 * g + 4, :] = value
    rows_ref[3:4, :] = jnp.ones((1, size), F32)
    rows_ref[12:16, :] = jnp.zeros((4, size), F32)
    side_ref[...] = rows_ref[0:16, :].astype(BF16)
    for b in range(tiles):
        at = slice(128 * b, 128 * (b + 1))
        square_ref[at, :] = jnp.dot(mine_ref[at, :], near_ref[...], preferred_element_type=F32)

    index = low_ref[...]
    low_ref[...] = index & 127
    unit_ref[...] = jnp.int32(1) << ((index >> 7) << 3)
    rows = lax.broadcasted_iota(jnp.int32, (128, 128), 0)

    def count(b):
        lanes = slice(128 * b, 128 * (b + 1))
        total = jnp.zeros((128, 128), jnp.int32)
        for k in range(neighbours):
            total += jnp.where(rows == low_ref[k : k + 1, lanes], unit_ref[k : k + 1, lanes], 0)
        count_ref[lanes, :] = jnp.transpose(total)

    step = 16

    def pairs(b):
        for s in range(height // step):
            here = slice(height * b + step * s, height * b + step * (s + 1))
            packed = count_ref[here, :]
            times = jnp.concatenate(
                [(packed >> (8 * f)) & 255 for f in range(tiles)], axis=1
            ).astype(F32)
            near = jnp.minimum(square_ref[here, :], RADIUS * RADIUS)
            u = near * (1.0 / (RADIUS * RADIUS))
            series = COSINE[4]
            for value in COSINE[3::-1]:
                series = series * u + value
            root = (1.0 - u) * series
            envelope = root * root * times
            pull_ref[here, :] = envelope
            distance = near * lax.rsqrt(near)
            growth = jnp.exp(distance * (4.0 * RADIUS / basis_count))
            basis = jnp.exp(near * -2.0) * envelope
            for n in range(basis_count):
                first = height * n + step * s
                basis_ref[b, first : first + step, :] = basis.astype(BF16)
                if n + 1 < basis_count:
                    basis = basis * growth

    number = lax.broadcasted_iota(jnp.int32, (basis_count, channels), 0).astype(F32)
    center = number * (RADIUS / basis_count)
    scale = jnp.exp(center * center * -2.0) * (1.0 / math.sqrt(neighbours))

    def gather(b, mixed, radial):
        every = jnp.dot(basis_ref[b], mixed, preferred_element_type=F32)
        message = radial[0:1] * every[0:height]
        for n in range(1, basis_count):
            message += radial[n : n + 1] * every[height * n : height * (n + 1)]
        active_ref[height * b : height * (b + 1), :] = jax.nn.silu(message).astype(BF16)

    def update(layer):
        change = jnp.dot(active_ref[...], out_w_ref[layer], preferred_element_type=F32)
        hidden_ref[...] = (hidden_ref[...].astype(F32) + change).astype(BF16)

    radial = radial_ref[0] * scale
    for b in range(blocks):
        if b % (128 // height) == 0:
            count(b // (128 // height))
        pairs(b)
        if b > 0:
            gather(b - 1, mixed, radial)
    gather(blocks - 1, mixed, radial)
    update(0)
    for layer in range(1, layers):
        mixed = mix(layer)
        radial = radial_ref[layer] * scale
        for b in range(blocks):
            gather(b, mixed, radial)
        update(layer)

    start = pl.multiple_of(half_ref[0] * own, own)
    key = jnp.dot(
        hidden_ref[...], read_ref[:, channels:], preferred_element_type=F32
    ).astype(BF16)
    query = jnp.dot(
        hidden_ref[pl.ds(start, own), :], read_ref[:, :channels], preferred_element_type=F32
    ).astype(BF16)
    across = (((1,), (1,)), ((), ()))
    side = side_ref[...]
    force_ref[...] = jnp.zeros_like(force_ref)
    for part in range(own // 128):
        here = pl.ds(start + 128 * part, 128)
        pull = lax.dot_general(
            query[128 * part : 128 * (part + 1)], key, across, preferred_element_type=F32
        ) * (pull_ref[here, :] * (1.0 / channels))
        high = pull.astype(BF16)
        rest = (pull - high.astype(F32)).astype(BF16)
        total = lax.dot_general(high, side, across, preferred_element_type=F32)
        total += lax.dot_general(rest, side, across, preferred_element_type=F32)
        turned = jnp.transpose(total)
        sums = turned[0:4] + turned[4:8] + turned[8:12]
        force = sums[0:3] - pos_ref[0:3, here] * sums[3:4]
        for a in range(128 // share):
            force_ref[128 // share * part + a, 0:3, 0:share] = force[:, share * a : share * (a + 1)]


def pair_kernel(
    tiles_ref,
    own_ref,
    low_ref,
    high_ref,
    force_ref,
    rows_ref,
    value_ref,
    near_ref,
    side_ref,
    mine_ref,
):
    listed, tiles = tiles_ref.shape
    for which, ref in enumerate((low_ref, own_ref, high_ref)):
        place = ref[...]
        pieces = split(place)
        norm = norm_of(place)
        right_rows(rows_ref, pieces, norm)
        charge = place[3:4]
        weighted = jnp.concatenate([place[0:3] * charge, charge], axis=0)
        for g, value in enumerate(split(weighted)):
            value_ref[4 * g : 4 * g + 4, :] = value
        value_ref[12:16, :] = jnp.zeros_like(place)
        for t in range(tiles):
            lanes = slice(TILE * t, TILE * (t + 1))
            near_ref[which * tiles + t] = rows_ref[:, lanes].astype(BF16)
            side_ref[which * tiles + t] = value_ref[:, lanes].astype(BF16)
    place = own_ref[...]
    is_place = lax.broadcasted_iota(jnp.int32, place.shape, 0) < 3
    left_rows(rows_ref, [jnp.where(is_place, piece, 0.0) for piece in split(place)], norm_of(place))
    for t in range(tiles):
        lanes = slice(TILE * t, TILE * (t + 1))
        mine_ref[lanes, :] = jnp.transpose(rows_ref[:, lanes]).astype(BF16)
    across = (((1,), (1,)), ((), ()))
    for t in range(tiles):
        lanes = slice(TILE * t, TILE * (t + 1))
        mine = mine_ref[lanes, :]
        total = jnp.zeros((TILE, 16), F32)
        for c in range(0, listed, 2):
            first, second = tiles_ref[c, t], tiles_ref[c + 1, t]
            squared = jnp.dot(
                mine,
                jnp.concatenate([near_ref[first], near_ref[second]], axis=1),
                preferred_element_type=F32,
            )
            inverse = lax.rsqrt(squared)
            total += lax.dot_general(
                (inverse * inverse * inverse).astype(BF16),
                jnp.concatenate([side_ref[first], side_ref[second]], axis=1),
                across,
                preferred_element_type=F32,
            )
        turned = jnp.transpose(total)
        sums = turned[0:4] + turned[4:8] + turned[8:12]
        place = own_ref[:, lanes]
        force_ref[:, lanes] = (place[0:3] * sums[3:4] - sums[0:3]) * (place[3:4] * COULOMB)


def vmem(count):
    return [pl.BlockSpec(memory_space=pltpu.VMEM)] * count


def on_device(
    mm_positions,
    mm_charge,
    mm_tiles,
    ml_feat,
    ml_positions,
    ml_neighbours,
    msg_weight,
    radial_weight,
    out_weight,
    read_weight,
):
    patches, share, channels = ml_feat.shape
    atom_count = mm_positions.shape[1]
    tile_count, listed = mm_tiles.shape
    members = lax.axis_size("ml")
    size = members * share
    own = size // HALVES
    neighbours = ml_neighbours.shape[1]
    basis_count = radial_weight.shape[1]
    limit = 48 * 1024 * 1024

    send, atoms = pl.pallas_call(
        pack_kernel,
        out_shape=(
            jax.ShapeDtypeStruct((members, share + 16, channels), BF16),
            jax.ShapeDtypeStruct((4, atom_count), F32),
        ),
        in_specs=vmem(5),
        out_specs=tuple(vmem(2)),
        scratch_shapes=[pltpu.VMEM((patches, 16, 128), F32)],
        cost_estimate=pl.CostEstimate(flops=1000, bytes_accessed=400000, transcendentals=0),
    )(
        ml_feat,
        ml_positions.transpose(1, 0, 2),
        ml_neighbours,
        mm_positions,
        mm_charge.reshape(1, atom_count),
    )
    recv = lax.all_to_all(send, "ml", split_axis=0, concat_axis=0, tiled=True)

    devices = lax.axis_size(("dom", "ml"))
    forward = [(i, (i + 1) % devices) for i in range(devices)]
    backward = [(b, a) for a, b in forward]
    low = lax.ppermute(atoms, ("dom", "ml"), forward)
    high = lax.ppermute(atoms, ("dom", "ml"), backward)

    half = (lax.axis_index("ml") // patches).astype(jnp.int32).reshape(1)
    forces = pl.pallas_call(
        patch_kernel,
        out_shape=jax.ShapeDtypeStruct((own // share, 8, 128), F32),
        in_specs=[pl.BlockSpec(memory_space=pltpu.SMEM)] + vmem(5),
        out_specs=vmem(1)[0],
        scratch_shapes=[
            pltpu.VMEM((size, channels), BF16),
            pltpu.VMEM((8, size), F32),
            pltpu.VMEM((32, size), F32),
            pltpu.VMEM((32, size), BF16),
            pltpu.VMEM((size, 32), BF16),
            pltpu.VMEM((16, size), BF16),
            pltpu.VMEM((neighbours, size), jnp.int32),
            pltpu.VMEM((neighbours, size), jnp.int32),
            pltpu.VMEM((size, 128), jnp.int32),
            pltpu.VMEM((size, size), F32),
            pltpu.VMEM((size // 64, basis_count * 64, size), BF16),
            pltpu.VMEM((size, size), F32),
            pltpu.VMEM((size, channels), BF16),
        ],
        compiler_params=pltpu.CompilerParams(vmem_limit_bytes=limit),
        cost_estimate=pl.CostEstimate(
            flops=5 * 10**9, bytes_accessed=1000000, transcendentals=10**6
        ),
    )(half, recv, msg_weight, radial_weight, out_weight, read_weight)
    groups = [[h * patches + p for p in range(patches)] for h in range(HALVES)]
    returned = lax.all_to_all(
        forces, "ml", split_axis=0, concat_axis=0, tiled=True, axis_index_groups=groups
    )
    ml_force = returned[:, :3, :share]

    mm_force = pl.pallas_call(
        pair_kernel,
        out_shape=jax.ShapeDtypeStruct((3, atom_count), F32),
        in_specs=[pl.BlockSpec(memory_space=pltpu.SMEM)] + vmem(3),
        out_specs=vmem(1)[0],
        scratch_shapes=[
            pltpu.VMEM((32, atom_count), F32),
            pltpu.VMEM((16, atom_count), F32),
            pltpu.VMEM((3 * tile_count, 32, TILE), BF16),
            pltpu.VMEM((3 * tile_count, 16, TILE), BF16),
            pltpu.VMEM((atom_count, 32), BF16),
        ],
        compiler_params=pltpu.CompilerParams(vmem_limit_bytes=limit),
        cost_estimate=pl.CostEstimate(
            flops=4 * 10**9, bytes_accessed=200000, transcendentals=10**6
        ),
    )(mm_tiles.T, atoms, low, high)
    return (mm_force, ml_force)


def solution(mesh):
    in_specs = (
        P(None, ("dom", "ml")),
        P(("dom", "ml")),
        P(("dom", "ml"), None),
        P("dom", "ml", None),
        P("dom", None, "ml"),
        P("dom", None, "ml"),
        P(),
        P(),
        P(),
        P(),
    )
    out_specs = (P(None, ("dom", "ml")), P("dom", None, "ml"))
    return jax.shard_map(
        on_device, mesh=mesh, in_specs=in_specs, out_specs=out_specs, check_vma=False
    )
```

```python
import math

import jax
import jax.numpy as jnp
from jax import lax
from jax.experimental import pallas as pl
from jax.experimental.pallas import tpu as pltpu
from jax.sharding import PartitionSpec as P

TILE = 128
RADIUS = 6.0
SOFTEN = 1.0
COULOMB = 0.5
HALVES = 2


def exchange_order(count):
    return list(range(count))[::-1]


COSINE = (
    0.9999999991255941,
    -0.23370050635000697,
    0.019968606683524803,
    -0.0008935362638784474,
    2.3601070666008123e-05,
)

F32 = jnp.float32
BF16 = jnp.bfloat16


def split(value):
    high = value.astype(BF16).astype(F32)
    rest = value - high
    middle = rest.astype(BF16).astype(F32)
    return high, middle, rest - middle


LEFT = (0, 0, 1, 1, 0, 2)
RIGHT = (0, 1, 0, 1, 2, 0)


def left_rows(rows_ref, pieces, norm):
    for g, which in enumerate(LEFT):
        rows_ref[4 * g : 4 * g + 4, :] = pieces[which]
    for g, value in enumerate(split(norm + SOFTEN)):
        rows_ref[24 + g : 25 + g, :] = value
    rows_ref[27:30, :] = jnp.ones((3, norm.shape[1]), F32)
    rows_ref[30:32, :] = jnp.zeros((2, norm.shape[1]), F32)


def right_rows(rows_ref, pieces, norm):
    for g, which in enumerate(RIGHT):
        rows_ref[4 * g : 4 * g + 4, :] = pieces[which] * -2.0
    rows_ref[24:27, :] = jnp.ones((3, norm.shape[1]), F32)
    for g, value in enumerate(split(norm)):
        rows_ref[27 + g : 28 + g, :] = value
    rows_ref[30:32, :] = jnp.zeros((2, norm.shape[1]), F32)


def norm_of(place):
    return place[0:1] * place[0:1] + place[1:2] * place[1:2] + place[2:3] * place[2:3]


def pack_kernel(feat_ref, pos_ref, nb_ref, mm_pos_ref, mm_charge_ref, send_ref, atoms_ref, geo_ref):
    patches, atoms, _ = feat_ref.shape
    members = send_ref.shape[0]
    holder = exchange_order(patches)
    geo_ref[...] = jnp.zeros_like(geo_ref)
    high, middle, low = split(pos_ref[...])
    for p in range(patches):
        numbers = (nb_ref[p] - 256).astype(F32)
        geo_ref[p, 0:16, 0:32] = numbers[0:16]
        geo_ref[p, 0:16, 32:64] = numbers[16:32]
        for axis in range(3):
            geo_ref[p, axis : axis + 1, 64:96] = high[axis, p : p + 1]
            geo_ref[p, axis : axis + 1, 96:128] = middle[axis, p : p + 1]
            geo_ref[p, axis + 8 : axis + 9, 64:96] = low[axis, p : p + 1]
        block = geo_ref[p].astype(BF16)
        for place, member in enumerate(exchange_order(members)):
            if member % patches == holder[p]:
                send_ref[place, 0:atoms, :] = feat_ref[p]
                send_ref[place, atoms : atoms + 16, :] = block
    atoms_ref[0:3, :] = mm_pos_ref[...]
    atoms_ref[3:4, :] = mm_charge_ref[...]


def patch_kernel(
    half_ref,
    recv_ref,
    msg_ref,
    radial_ref,
    out_w_ref,
    read_ref,
    force_ref,
    hidden_ref,
    pos_ref,
    rows_ref,
    near_ref,
    mine_ref,
    side_ref,
    low_ref,
    unit_ref,
    count_ref,
    square_ref,
    basis_ref,
    pull_ref,
    active_ref,
):
    sources = recv_ref.shape[0]
    share = recv_ref.shape[1] - 16
    size = sources * share
    own = size // HALVES
    neighbours = low_ref.shape[0]
    basis_count = radial_ref.shape[1]
    layers = msg_ref.shape[0]
    channels = recv_ref.shape[2]
    blocks = basis_ref.shape[0]
    height = size // blocks
    tiles = size // 128

    for place, m in enumerate(exchange_order(sources)):
        hidden_ref[share * m : share * (m + 1), :] = recv_ref[place, 0:share, :]
        geo = recv_ref[place, share : share + 16, :].astype(F32)
        lanes = slice(share * m, share * (m + 1))
        pos_ref[:, lanes] = (geo[0:8, 64:96] + geo[0:8, 96:128]) + geo[8:16, 64:96]
        low_ref[0:16, lanes] = geo[:, 0:32].astype(jnp.int32) + 256
        low_ref[16:32, lanes] = geo[:, 32:64].astype(jnp.int32) + 256

    def mix(layer):
        return jnp.dot(hidden_ref[...], msg_ref[layer], preferred_element_type=F32).astype(BF16)

    mixed = mix(0)

    place = pos_ref[0:4, :]
    pieces = split(place)
    norm = norm_of(place)
    right_rows(rows_ref, pieces, norm)
    near_ref[...] = rows_ref[...].astype(BF16)
    left_rows(rows_ref, pieces, norm)
    for b in range(tiles):
        at = slice(128 * b, 128 * (b + 1))
        mine_ref[at, :] = jnp.transpose(rows_ref[:, at]).astype(BF16)
    for g, value in enumerate(pieces):
        rows_ref[4 * g : 4 * g + 4, :] = value
    rows_ref[3:4, :] = jnp.ones((1, size), F32)
    rows_ref[12:16, :] = jnp.zeros((4, size), F32)
    side_ref[...] = rows_ref[0:16, :].astype(BF16)
    for b in range(tiles):
        at = slice(128 * b, 128 * (b + 1))
        square_ref[at, :] = jnp.dot(mine_ref[at, :], near_ref[...], preferred_element_type=F32)

    index = low_ref[...]
    low_ref[...] = index & 127
    unit_ref[...] = jnp.int32(1) << ((index >> 7) << 3)
    rows = lax.broadcasted_iota(jnp.int32, (128, 128), 0)

    def count(b):
        lanes = slice(128 * b, 128 * (b + 1))
        total = jnp.zeros((128, 128), jnp.int32)
        for k in range(neighbours):
            total += jnp.where(rows == low_ref[k : k + 1, lanes], unit_ref[k : k + 1, lanes], 0)
        count_ref[lanes, :] = jnp.transpose(total)

    step = 16

    def pairs(b):
        for s in range(height // step):
            here = slice(height * b + step * s, height * b + step * (s + 1))
            packed = count_ref[here, :]
            times = jnp.concatenate(
                [(packed >> (8 * f)) & 255 for f in range(tiles)], axis=1
            ).astype(F32)
            near = jnp.minimum(square_ref[here, :], RADIUS * RADIUS)
            u = near * (1.0 / (RADIUS * RADIUS))
            series = COSINE[4]
            for value in COSINE[3::-1]:
                series = series * u + value
            root = (1.0 - u) * series
            envelope = root * root * times
            pull_ref[here, :] = envelope
            distance = near * lax.rsqrt(near)
            growth = jnp.exp(distance * (4.0 * RADIUS / basis_count))
            basis = jnp.exp(near * -2.0) * envelope
            for n in range(basis_count):
                first = height * n + step * s
                basis_ref[b, first : first + step, :] = basis.astype(BF16)
                if n + 1 < basis_count:
                    basis = basis * growth

    number = lax.broadcasted_iota(jnp.int32, (basis_count, channels), 0).astype(F32)
    center = number * (RADIUS / basis_count)
    scale = jnp.exp(center * center * -2.0) * (1.0 / math.sqrt(neighbours))

    def gather(b, mixed, radial):
        every = jnp.dot(basis_ref[b], mixed, preferred_element_type=F32)
        message = radial[0:1] * every[0:height]
        for n in range(1, basis_count):
            message += radial[n : n + 1] * every[height * n : height * (n + 1)]
        active_ref[height * b : height * (b + 1), :] = jax.nn.silu(message).astype(BF16)

    def update(layer):
        change = jnp.dot(active_ref[...], out_w_ref[layer], preferred_element_type=F32)
        hidden_ref[...] = (hidden_ref[...].astype(F32) + change).astype(BF16)

    radial = radial_ref[0] * scale
    for b in range(blocks):
        if b % (128 // height) == 0:
            count(b // (128 // height))
        pairs(b)
        if b > 0:
            gather(b - 1, mixed, radial)
    gather(blocks - 1, mixed, radial)
    update(0)
    for layer in range(1, layers):
        mixed = mix(layer)
        radial = radial_ref[layer] * scale
        for b in range(blocks):
            gather(b, mixed, radial)
        update(layer)

    start = pl.multiple_of(half_ref[0] * own, own)
    key = jnp.dot(
        hidden_ref[...], read_ref[:, channels:], preferred_element_type=F32
    ).astype(BF16)
    query = jnp.dot(
        hidden_ref[pl.ds(start, own), :], read_ref[:, :channels], preferred_element_type=F32
    ).astype(BF16)
    across = (((1,), (1,)), ((), ()))
    order = exchange_order(own // share)
    side = side_ref[...]
    force_ref[...] = jnp.zeros_like(force_ref)
    for part in range(own // 128):
        here = pl.ds(start + 128 * part, 128)
        pull = lax.dot_general(
            query[128 * part : 128 * (part + 1)], key, across, preferred_element_type=F32
        ) * (pull_ref[here, :] * (1.0 / channels))
        high = pull.astype(BF16)
        rest = (pull - high.astype(F32)).astype(BF16)
        total = lax.dot_general(high, side, across, preferred_element_type=F32)
        total += lax.dot_general(rest, side, across, preferred_element_type=F32)
        turned = jnp.transpose(total)
        sums = turned[0:4] + turned[4:8] + turned[8:12]
        force = sums[0:3] - pos_ref[0:3, here] * sums[3:4]
        for a in range(128 // share):
            place = order.index(128 // share * part + a)
            force_ref[place, 0:3, 0:share] = force[:, share * a : share * (a + 1)]


def pair_kernel(
    tiles_ref,
    own_ref,
    low_ref,
    high_ref,
    force_ref,
    rows_ref,
    value_ref,
    near_ref,
    side_ref,
    mine_ref,
):
    listed, tiles = tiles_ref.shape
    for which, ref in enumerate((low_ref, own_ref, high_ref)):
        place = ref[...]
        pieces = split(place)
        norm = norm_of(place)
        right_rows(rows_ref, pieces, norm)
        charge = place[3:4]
        weighted = jnp.concatenate([place[0:3] * charge, charge], axis=0)
        for g, value in enumerate(split(weighted)):
            value_ref[4 * g : 4 * g + 4, :] = value
        value_ref[12:16, :] = jnp.zeros_like(place)
        for t in range(tiles):
            lanes = slice(TILE * t, TILE * (t + 1))
            near_ref[which * tiles + t] = rows_ref[:, lanes].astype(BF16)
            side_ref[which * tiles + t] = value_ref[:, lanes].astype(BF16)
    place = own_ref[...]
    is_place = lax.broadcasted_iota(jnp.int32, place.shape, 0) < 3
    left_rows(rows_ref, [jnp.where(is_place, piece, 0.0) for piece in split(place)], norm_of(place))
    for t in range(tiles):
        lanes = slice(TILE * t, TILE * (t + 1))
        mine_ref[lanes, :] = jnp.transpose(rows_ref[:, lanes]).astype(BF16)
    across = (((1,), (1,)), ((), ()))
    for t in range(tiles):
        lanes = slice(TILE * t, TILE * (t + 1))
        mine = mine_ref[lanes, :]
        total = jnp.zeros((TILE, 16), F32)
        for c in range(0, listed, 2):
            first, second = tiles_ref[c, t], tiles_ref[c + 1, t]
            squared = jnp.dot(
                mine,
                jnp.concatenate([near_ref[first], near_ref[second]], axis=1),
                preferred_element_type=F32,
            )
            inverse = lax.rsqrt(squared)
            total += lax.dot_general(
                (inverse * inverse * inverse).astype(BF16),
                jnp.concatenate([side_ref[first], side_ref[second]], axis=1),
                across,
                preferred_element_type=F32,
            )
        turned = jnp.transpose(total)
        sums = turned[0:4] + turned[4:8] + turned[8:12]
        place = own_ref[:, lanes]
        force_ref[:, lanes] = (place[0:3] * sums[3:4] - sums[0:3]) * (place[3:4] * COULOMB)


def vmem(count):
    return [pl.BlockSpec(memory_space=pltpu.VMEM)] * count


def on_device(
    mm_positions,
    mm_charge,
    mm_tiles,
    ml_feat,
    ml_positions,
    ml_neighbours,
    msg_weight,
    radial_weight,
    out_weight,
    read_weight,
):
    patches, share, channels = ml_feat.shape
    atom_count = mm_positions.shape[1]
    tile_count, listed = mm_tiles.shape
    members = lax.axis_size("ml")
    size = members * share
    own = size // HALVES
    neighbours = ml_neighbours.shape[1]
    basis_count = radial_weight.shape[1]
    limit = 48 * 1024 * 1024

    send, atoms = pl.pallas_call(
        pack_kernel,
        out_shape=(
            jax.ShapeDtypeStruct((members, share + 16, channels), BF16),
            jax.ShapeDtypeStruct((4, atom_count), F32),
        ),
        in_specs=vmem(5),
        out_specs=tuple(vmem(2)),
        scratch_shapes=[pltpu.VMEM((patches, 16, 128), F32)],
        cost_estimate=pl.CostEstimate(flops=1000, bytes_accessed=400000, transcendentals=0),
    )(
        ml_feat,
        ml_positions.transpose(1, 0, 2),
        ml_neighbours,
        mm_positions,
        mm_charge.reshape(1, atom_count),
    )
    recv = lax.all_to_all(
        send,
        "ml",
        split_axis=0,
        concat_axis=0,
        tiled=True,
        axis_index_groups=[exchange_order(members)],
    )

    devices = lax.axis_size(("dom", "ml"))
    forward = [(i, (i + 1) % devices) for i in range(devices)]
    backward = [(b, a) for a, b in forward]
    low = lax.ppermute(atoms, ("dom", "ml"), forward)
    high = lax.ppermute(atoms, ("dom", "ml"), backward)

    half = (lax.axis_index("ml") // patches).astype(jnp.int32).reshape(1)
    forces = pl.pallas_call(
        patch_kernel,
        out_shape=jax.ShapeDtypeStruct((own // share, 8, 128), F32),
        in_specs=[pl.BlockSpec(memory_space=pltpu.SMEM)] + vmem(5),
        out_specs=vmem(1)[0],
        scratch_shapes=[
            pltpu.VMEM((size, channels), BF16),
            pltpu.VMEM((8, size), F32),
            pltpu.VMEM((32, size), F32),
            pltpu.VMEM((32, size), BF16),
            pltpu.VMEM((size, 32), BF16),
            pltpu.VMEM((16, size), BF16),
            pltpu.VMEM((neighbours, size), jnp.int32),
            pltpu.VMEM((neighbours, size), jnp.int32),
            pltpu.VMEM((size, 128), jnp.int32),
            pltpu.VMEM((size, size), F32),
            pltpu.VMEM((size // 64, basis_count * 64, size), BF16),
            pltpu.VMEM((size, size), F32),
            pltpu.VMEM((size, channels), BF16),
        ],
        compiler_params=pltpu.CompilerParams(vmem_limit_bytes=limit),
        cost_estimate=pl.CostEstimate(
            flops=5 * 10**9, bytes_accessed=1000000, transcendentals=10**6
        ),
    )(half, recv, msg_weight, radial_weight, out_weight, read_weight)
    groups = [[h * patches + p for p in exchange_order(patches)] for h in range(HALVES)]
    returned = lax.all_to_all(
        forces, "ml", split_axis=0, concat_axis=0, tiled=True, axis_index_groups=groups
    )
    ml_force = returned[:, :3, :share]

    mm_force = pl.pallas_call(
        pair_kernel,
        out_shape=jax.ShapeDtypeStruct((3, atom_count), F32),
        in_specs=[pl.BlockSpec(memory_space=pltpu.SMEM)] + vmem(3),
        out_specs=vmem(1)[0],
        scratch_shapes=[
            pltpu.VMEM((32, atom_count), F32),
            pltpu.VMEM((16, atom_count), F32),
            pltpu.VMEM((3 * tile_count, 32, TILE), BF16),
            pltpu.VMEM((3 * tile_count, 16, TILE), BF16),
            pltpu.VMEM((atom_count, 32), BF16),
        ],
        compiler_params=pltpu.CompilerParams(vmem_limit_bytes=limit),
        cost_estimate=pl.CostEstimate(
            flops=4 * 10**9, bytes_accessed=200000, transcendentals=10**6
        ),
    )(mm_tiles.T, atoms, low, high)
    return (mm_force, ml_force)


def solution(mesh):
    in_specs = (
        P(None, ("dom", "ml")),
        P(("dom", "ml")),
        P(("dom", "ml"), None),
        P("dom", "ml", None),
        P("dom", None, "ml"),
        P("dom", None, "ml"),
        P(),
        P(),
        P(),
        P(),
    )
    out_specs = (P(None, ("dom", "ml")), P("dom", None, "ml"))
    return jax.shard_map(
        on_device, mesh=mesh, in_specs=in_specs, out_specs=out_specs, check_vma=False
    )
```

```python
import math

import jax
import jax.numpy as jnp
from jax import lax
from jax.experimental import pallas as pl
from jax.experimental.pallas import tpu as pltpu
from jax.sharding import PartitionSpec as P

TILE = 128
RADIUS = 6.0
SOFTEN = 1.0
COULOMB = 0.5
HALVES = 2


def exchange_order(count):
    return list(range(count))[::-1]


COSINE = (
    0.9999999991255941,
    -0.23370050635000697,
    0.019968606683524803,
    -0.0008935362638784474,
    2.3601070666008123e-05,
)

F32 = jnp.float32
BF16 = jnp.bfloat16


def split(value):
    high = value.astype(BF16).astype(F32)
    rest = value - high
    middle = rest.astype(BF16).astype(F32)
    return high, middle, rest - middle


LEFT = (0, 0, 1, 1, 0, 2)
RIGHT = (0, 1, 0, 1, 2, 0)


def left_rows(rows_ref, pieces, norm):
    for g, which in enumerate(LEFT):
        rows_ref[4 * g : 4 * g + 4, :] = pieces[which]
    for g, value in enumerate(split(norm + SOFTEN)):
        rows_ref[24 + g : 25 + g, :] = value
    rows_ref[27:30, :] = jnp.ones((3, norm.shape[1]), F32)
    rows_ref[30:32, :] = jnp.zeros((2, norm.shape[1]), F32)


def right_rows(rows_ref, pieces, norm):
    for g, which in enumerate(RIGHT):
        rows_ref[4 * g : 4 * g + 4, :] = pieces[which] * -2.0
    rows_ref[24:27, :] = jnp.ones((3, norm.shape[1]), F32)
    for g, value in enumerate(split(norm)):
        rows_ref[27 + g : 28 + g, :] = value
    rows_ref[30:32, :] = jnp.zeros((2, norm.shape[1]), F32)


def norm_of(place):
    return place[0:1] * place[0:1] + place[1:2] * place[1:2] + place[2:3] * place[2:3]


def pack_kernel(feat_ref, pos_ref, nb_ref, mm_pos_ref, mm_charge_ref, send_ref, atoms_ref, geo_ref):
    patches, atoms, _ = feat_ref.shape
    members = send_ref.shape[0]
    holder = exchange_order(patches)
    geo_ref[...] = jnp.zeros_like(geo_ref)
    high, middle, low = split(pos_ref[...])
    for p in range(patches):
        numbers = (nb_ref[p] - 256).astype(F32)
        geo_ref[p, 0:16, 0:32] = numbers[0:16]
        geo_ref[p, 0:16, 32:64] = numbers[16:32]
        for axis in range(3):
            geo_ref[p, axis : axis + 1, 64:96] = high[axis, p : p + 1]
            geo_ref[p, axis : axis + 1, 96:128] = middle[axis, p : p + 1]
            geo_ref[p, axis + 8 : axis + 9, 64:96] = low[axis, p : p + 1]
        block = geo_ref[p].astype(BF16)
        for place, member in enumerate(exchange_order(members)):
            if member % patches == holder[p]:
                send_ref[place, 0:atoms, :] = feat_ref[p]
                send_ref[place, atoms : atoms + 16, :] = block
    atoms_ref[0:3, :] = mm_pos_ref[...]
    atoms_ref[3:4, :] = mm_charge_ref[...]


def patch_kernel(
    half_ref,
    recv_ref,
    msg_ref,
    radial_ref,
    out_w_ref,
    read_ref,
    force_ref,
    plain_ref,
    hidden_ref,
    pos_ref,
    rows_ref,
    near_ref,
    mine_ref,
    side_ref,
    low_ref,
    unit_ref,
    count_ref,
    square_ref,
    basis_ref,
    pull_ref,
):
    sources = recv_ref.shape[0]
    share = recv_ref.shape[1] - 16
    size = sources * share
    own = size // HALVES
    neighbours = low_ref.shape[0]
    basis_count = radial_ref.shape[1]
    layers = msg_ref.shape[0]
    channels = recv_ref.shape[2]
    tiles = size // 128

    for place, m in enumerate(exchange_order(sources)):
        plain_ref[share * m : share * (m + 1), :] = recv_ref[place, 0:share, :]
        geo = recv_ref[place, share : share + 16, :].astype(F32)
        lanes = slice(share * m, share * (m + 1))
        pos_ref[:, lanes] = (geo[0:8, 64:96] + geo[0:8, 96:128]) + geo[8:16, 64:96]
        low_ref[0:16, lanes] = geo[:, 0:32].astype(jnp.int32) + 256
        low_ref[16:32, lanes] = geo[:, 32:64].astype(jnp.int32) + 256
    hidden_ref[...] = jnp.transpose(plain_ref[...])
    msg = [jnp.transpose(msg_ref[layer]) for layer in range(layers)]
    out_w = [jnp.transpose(out_w_ref[layer]) for layer in range(layers)]
    read = jnp.transpose(read_ref[...])

    def mix(layer):
        return jnp.dot(msg[layer], hidden_ref[...], preferred_element_type=F32).astype(BF16)

    mixed = mix(0)

    place = pos_ref[0:4, :]
    pieces = split(place)
    norm = norm_of(place)
    right_rows(rows_ref, pieces, norm)
    near_ref[...] = rows_ref[...].astype(BF16)
    left_rows(rows_ref, pieces, norm)
    for b in range(tiles):
        at = slice(128 * b, 128 * (b + 1))
        mine_ref[at, :] = jnp.transpose(rows_ref[:, at]).astype(BF16)
    for g, value in enumerate(pieces):
        rows_ref[4 * g : 4 * g + 4, :] = value
    rows_ref[3:4, :] = jnp.ones((1, size), F32)
    rows_ref[12:16, :] = jnp.zeros((4, size), F32)
    side_ref[...] = rows_ref[0:16, :].astype(BF16)
    square_ref[...] = jnp.dot(mine_ref[...], near_ref[...], preferred_element_type=F32)

    index = low_ref[...]
    low_ref[...] = index & 127
    unit_ref[...] = jnp.int32(1) << ((index >> 7) << 3)
    rows = lax.broadcasted_iota(jnp.int32, (128, 128), 0)

    def count(b):
        lanes = slice(128 * b, 128 * (b + 1))
        total = jnp.zeros((128, 128), jnp.int32)
        for k in range(neighbours):
            total += jnp.where(rows == low_ref[k : k + 1, lanes], unit_ref[k : k + 1, lanes], 0)
        count_ref[:, lanes] = total

    step = 32
    limit = RADIUS * RADIUS
    per_basis = 4.0 * RADIUS / basis_count / math.log(2.0)
    series = [value / limit ** (k + 1) for k, value in enumerate(COSINE)]

    def pairs(lanes):
        for s in range(size // step):
            here = slice(step * s, step * (s + 1))
            f, first = divmod(step * s, 128)
            times = ((count_ref[first : first + step, lanes] >> (8 * f)) & 255).astype(F32)
            near = jnp.minimum(square_ref[here, lanes], limit)
            root = series[-1]
            for value in series[-2::-1]:
                root = root * near + value
            root = (limit - near) * root
            envelope = root * root * times
            pull_ref[here, lanes] = envelope
            growth = jnp.exp2(near * lax.rsqrt(near) * per_basis)
            basis = jnp.exp2(near * (-2.0 / math.log(2.0))) * envelope
            for n in range(basis_count):
                basis_ref[n, here, lanes] = basis.astype(BF16)
                if n + 1 < basis_count:
                    basis = basis * growth

    number = lax.broadcasted_iota(jnp.int32, (basis_count, channels), 0).astype(F32)
    center = number * (RADIUS / basis_count)
    scale = jnp.exp(center * center * -2.0) * (1.0 / math.sqrt(neighbours))
    radial = [jnp.transpose(radial_ref[layer] * scale) for layer in range(layers)]

    def advance(layer, lanes, mixed):
        message = 0.0
        for n in range(basis_count):
            message += radial[layer][:, n : n + 1] * jnp.dot(
                mixed, basis_ref[n, :, lanes], preferred_element_type=F32
            )
        active = jax.nn.silu(message).astype(BF16)
        change = jnp.dot(out_w[layer], active, preferred_element_type=F32)
        return (hidden_ref[:, lanes].astype(F32) + change).astype(BF16)

    parts = [slice(own * part, own * (part + 1)) for part in range(HALVES)]
    for part, lanes in enumerate(parts):
        for b in range(tiles // HALVES):
            count(tiles // HALVES * part + b)
        pairs(lanes)
    for layer in range(layers):
        if layer > 0:
            mixed = mix(layer)
        later = [advance(layer, lanes, mixed) for lanes in parts]
        for lanes, value in zip(parts, later):
            hidden_ref[:, lanes] = value

    mine = pl.ds(pl.multiple_of(half_ref[0] * own, own), own)
    key = jnp.transpose(
        jnp.dot(read[channels:], hidden_ref[...], preferred_element_type=F32)
    ).astype(BF16)
    query = jnp.dot(read[:channels], hidden_ref[:, mine], preferred_element_type=F32).astype(BF16)
    side = side_ref[...]
    total = jnp.zeros((16, own), F32)
    for here in parts:
        pull = jnp.dot(key[here], query, preferred_element_type=F32) * (
            pull_ref[here, mine] * (1.0 / channels)
        )
        high = pull.astype(BF16)
        rest = (pull - high.astype(F32)).astype(BF16)
        total += jnp.dot(side[:, here], high, preferred_element_type=F32)
        total += jnp.dot(side[:, here], rest, preferred_element_type=F32)
    sums = total[0:4] + total[4:8] + total[8:12]
    force = sums[0:3] - pos_ref[0:3, mine] * sums[3:4]
    force_ref[...] = jnp.zeros_like(force_ref)
    for place, a in enumerate(exchange_order(own // share)):
        force_ref[place, 0:3, 0:share] = force[:, share * a : share * (a + 1)]


def pair_kernel(
    tiles_ref,
    own_ref,
    low_ref,
    high_ref,
    force_ref,
    rows_ref,
    value_ref,
    near_ref,
    side_ref,
    mine_ref,
):
    listed, tiles = tiles_ref.shape
    for which, ref in enumerate((low_ref, own_ref, high_ref)):
        place = ref[...]
        pieces = split(place)
        norm = norm_of(place)
        right_rows(rows_ref, pieces, norm)
        charge = place[3:4]
        weighted = jnp.concatenate([place[0:3] * charge, charge], axis=0)
        for g, value in enumerate(split(weighted)):
            value_ref[4 * g : 4 * g + 4, :] = value
        value_ref[12:16, :] = jnp.zeros_like(place)
        for t in range(tiles):
            lanes = slice(TILE * t, TILE * (t + 1))
            near_ref[which * tiles + t] = rows_ref[:, lanes].astype(BF16)
            side_ref[which * tiles + t] = value_ref[:, lanes].astype(BF16)
    place = own_ref[...]
    is_place = lax.broadcasted_iota(jnp.int32, place.shape, 0) < 3
    left_rows(rows_ref, [jnp.where(is_place, piece, 0.0) for piece in split(place)], norm_of(place))
    for t in range(tiles):
        lanes = slice(TILE * t, TILE * (t + 1))
        mine_ref[lanes, :] = jnp.transpose(rows_ref[:, lanes]).astype(BF16)
    across = (((1,), (1,)), ((), ()))
    for t in range(tiles):
        lanes = slice(TILE * t, TILE * (t + 1))
        mine = mine_ref[lanes, :]
        total = jnp.zeros((TILE, 16), F32)
        for c in range(0, listed, 2):
            first, second = tiles_ref[c, t], tiles_ref[c + 1, t]
            squared = jnp.dot(
                mine,
                jnp.concatenate([near_ref[first], near_ref[second]], axis=1),
                preferred_element_type=F32,
            )
            inverse = lax.rsqrt(squared)
            total += lax.dot_general(
                (inverse * inverse * inverse).astype(BF16),
                jnp.concatenate([side_ref[first], side_ref[second]], axis=1),
                across,
                preferred_element_type=F32,
            )
        turned = jnp.transpose(total)
        sums = turned[0:4] + turned[4:8] + turned[8:12]
        place = own_ref[:, lanes]
        force_ref[:, lanes] = (place[0:3] * sums[3:4] - sums[0:3]) * (place[3:4] * COULOMB)


def vmem(count):
    return [pl.BlockSpec(memory_space=pltpu.VMEM)] * count


def on_device(
    mm_positions,
    mm_charge,
    mm_tiles,
    ml_feat,
    ml_positions,
    ml_neighbours,
    msg_weight,
    radial_weight,
    out_weight,
    read_weight,
):
    patches, share, channels = ml_feat.shape
    atom_count = mm_positions.shape[1]
    tile_count, listed = mm_tiles.shape
    members = lax.axis_size("ml")
    size = members * share
    own = size // HALVES
    neighbours = ml_neighbours.shape[1]
    basis_count = radial_weight.shape[1]
    limit = 48 * 1024 * 1024

    send, atoms = pl.pallas_call(
        pack_kernel,
        out_shape=(
            jax.ShapeDtypeStruct((members, share + 16, channels), BF16),
            jax.ShapeDtypeStruct((4, atom_count), F32),
        ),
        in_specs=vmem(5),
        out_specs=tuple(vmem(2)),
        scratch_shapes=[pltpu.VMEM((patches, 16, 128), F32)],
        cost_estimate=pl.CostEstimate(flops=1000, bytes_accessed=400000, transcendentals=0),
    )(
        ml_feat,
        ml_positions.transpose(1, 0, 2),
        ml_neighbours,
        mm_positions,
        mm_charge.reshape(1, atom_count),
    )
    recv = lax.all_to_all(
        send,
        "ml",
        split_axis=0,
        concat_axis=0,
        tiled=True,
        axis_index_groups=[exchange_order(members)],
    )

    devices = lax.axis_size(("dom", "ml"))
    forward = [(i, (i + 1) % devices) for i in range(devices)]
    backward = [(b, a) for a, b in forward]
    low = lax.ppermute(atoms, ("dom", "ml"), forward)
    high = lax.ppermute(atoms, ("dom", "ml"), backward)

    half = (lax.axis_index("ml") // patches).astype(jnp.int32).reshape(1)
    forces = pl.pallas_call(
        patch_kernel,
        out_shape=jax.ShapeDtypeStruct((own // share, 8, 128), F32),
        in_specs=[pl.BlockSpec(memory_space=pltpu.SMEM)] + vmem(5),
        out_specs=vmem(1)[0],
        scratch_shapes=[
            pltpu.VMEM((size, channels), BF16),
            pltpu.VMEM((channels, size), BF16),
            pltpu.VMEM((8, size), F32),
            pltpu.VMEM((32, size), F32),
            pltpu.VMEM((32, size), BF16),
            pltpu.VMEM((size, 32), BF16),
            pltpu.VMEM((16, size), BF16),
            pltpu.VMEM((neighbours, size), jnp.int32),
            pltpu.VMEM((neighbours, size), jnp.int32),
            pltpu.VMEM((128, size), jnp.int32),
            pltpu.VMEM((size, size), F32),
            pltpu.VMEM((basis_count, size, size), BF16),
            pltpu.VMEM((size, size), F32),
        ],
        compiler_params=pltpu.CompilerParams(vmem_limit_bytes=limit),
        cost_estimate=pl.CostEstimate(
            flops=5 * 10**9, bytes_accessed=1000000, transcendentals=10**6
        ),
    )(half, recv, msg_weight, radial_weight, out_weight, read_weight)
    groups = [[h * patches + p for p in exchange_order(patches)] for h in range(HALVES)]
    returned = lax.all_to_all(
        forces, "ml", split_axis=0, concat_axis=0, tiled=True, axis_index_groups=groups
    )
    ml_force = returned[:, :3, :share]

    mm_force = pl.pallas_call(
        pair_kernel,
        out_shape=jax.ShapeDtypeStruct((3, atom_count), F32),
        in_specs=[pl.BlockSpec(memory_space=pltpu.SMEM)] + vmem(3),
        out_specs=vmem(1)[0],
        scratch_shapes=[
            pltpu.VMEM((32, atom_count), F32),
            pltpu.VMEM((16, atom_count), F32),
            pltpu.VMEM((3 * tile_count, 32, TILE), BF16),
            pltpu.VMEM((3 * tile_count, 16, TILE), BF16),
            pltpu.VMEM((atom_count, 32), BF16),
        ],
        compiler_params=pltpu.CompilerParams(vmem_limit_bytes=limit),
        cost_estimate=pl.CostEstimate(
            flops=4 * 10**9, bytes_accessed=200000, transcendentals=10**6
        ),
    )(mm_tiles.T, atoms, low, high)
    return (mm_force, ml_force)


def solution(mesh):
    in_specs = (
        P(None, ("dom", "ml")),
        P(("dom", "ml")),
        P(("dom", "ml"), None),
        P("dom", "ml", None),
        P("dom", None, "ml"),
        P("dom", None, "ml"),
        P(),
        P(),
        P(),
        P(),
    )
    out_specs = (P(None, ("dom", "ml")), P("dom", None, "ml"))
    return jax.shard_map(
        on_device, mesh=mesh, in_specs=in_specs, out_specs=out_specs, check_vma=False
    )
```

```python
import math

import jax
import jax.numpy as jnp
from jax import lax
from jax.experimental import pallas as pl
from jax.experimental.pallas import tpu as pltpu
from jax.sharding import PartitionSpec as P

TILE = 128
RADIUS = 6.0
SOFTEN = 1.0
COULOMB = 0.5
HALVES = 2


FIRST = {16: 10, 8: 2}


def exchange_order(count):
    first = FIRST.get(count, count - 1)
    return [first] + [member for member in range(count)[::-1] if member != first]


COSINE = (
    0.9999999991255941,
    -0.23370050635000697,
    0.019968606683524803,
    -0.0008935362638784474,
    2.3601070666008123e-05,
)

F32 = jnp.float32
BF16 = jnp.bfloat16


def split(value):
    high = value.astype(BF16).astype(F32)
    rest = value - high
    middle = rest.astype(BF16).astype(F32)
    return high, middle, rest - middle


LEFT = (0, 0, 1, 1, 0, 2)
RIGHT = (0, 1, 0, 1, 2, 0)


def left_rows(rows_ref, pieces, norm):
    for g, which in enumerate(LEFT):
        rows_ref[4 * g : 4 * g + 4, :] = pieces[which]
    for g, value in enumerate(split(norm + SOFTEN)):
        rows_ref[24 + g : 25 + g, :] = value
    rows_ref[27:30, :] = jnp.ones((3, norm.shape[1]), F32)
    rows_ref[30:32, :] = jnp.zeros((2, norm.shape[1]), F32)


def right_rows(rows_ref, pieces, norm):
    for g, which in enumerate(RIGHT):
        rows_ref[4 * g : 4 * g + 4, :] = pieces[which] * -2.0
    rows_ref[24:27, :] = jnp.ones((3, norm.shape[1]), F32)
    for g, value in enumerate(split(norm)):
        rows_ref[27 + g : 28 + g, :] = value
    rows_ref[30:32, :] = jnp.zeros((2, norm.shape[1]), F32)


def norm_of(place):
    return place[0:1] * place[0:1] + place[1:2] * place[1:2] + place[2:3] * place[2:3]


def pack_kernel(
    feat_ref,
    pos_ref,
    nb_ref,
    mm_pos_ref,
    mm_charge_ref,
    radial_ref,
    send_ref,
    atoms_ref,
    near_radial_ref,
    geo_ref,
):
    patches, atoms, _ = feat_ref.shape
    members = send_ref.shape[0]
    holder = exchange_order(patches)
    geo_ref[...] = jnp.zeros_like(geo_ref)
    high, middle, low = split(pos_ref[...])
    for p in range(patches):
        numbers = (nb_ref[p] - 256).astype(F32)
        geo_ref[p, 0:16, 0:32] = numbers[0:16]
        geo_ref[p, 0:16, 32:64] = numbers[16:32]
        for axis in range(3):
            geo_ref[p, axis : axis + 1, 64:96] = high[axis, p : p + 1]
            geo_ref[p, axis : axis + 1, 96:128] = middle[axis, p : p + 1]
            geo_ref[p, axis + 8 : axis + 9, 64:96] = low[axis, p : p + 1]
        block = geo_ref[p].astype(BF16)
        for place, member in enumerate(exchange_order(members)):
            if member % patches == holder[p]:
                send_ref[place, 0:atoms, :] = feat_ref[p]
                send_ref[place, atoms : atoms + 16, :] = block
    atoms_ref[0:3, :] = mm_pos_ref[...]
    atoms_ref[3:4, :] = mm_charge_ref[...]
    near_radial_ref[...] = radial_ref[...]


def patch_kernel(
    recv_ref,
    msg_ref,
    radial_ref,
    out_w_ref,
    read_ref,
    force_ref,
    plain_ref,
    hidden_ref,
    pos_ref,
    rows_ref,
    near_ref,
    mine_ref,
    side_ref,
    low_ref,
    unit_ref,
    count_ref,
    square_ref,
    basis_ref,
    pull_ref,
):
    sources = recv_ref.shape[0]
    share = recv_ref.shape[1] - 16
    size = sources * share
    own = size // HALVES
    neighbours = low_ref.shape[0]
    basis_count = radial_ref.shape[1]
    layers = msg_ref.shape[0]
    channels = recv_ref.shape[2]
    tiles = size // 128

    for place, m in enumerate(exchange_order(sources)):
        plain_ref[share * m : share * (m + 1), :] = recv_ref[place, 0:share, :]
        geo = recv_ref[place, share : share + 16, :].astype(F32)
        lanes = slice(share * m, share * (m + 1))
        pos_ref[:, lanes] = (geo[0:8, 64:96] + geo[0:8, 96:128]) + geo[8:16, 64:96]
        low_ref[0:16, lanes] = geo[:, 0:32].astype(jnp.int32) + 256
        low_ref[16:32, lanes] = geo[:, 32:64].astype(jnp.int32) + 256
    hidden_ref[...] = jnp.transpose(plain_ref[...])
    msg = [jnp.transpose(msg_ref[layer]) for layer in range(layers)]
    out_w = [jnp.transpose(out_w_ref[layer]) for layer in range(layers)]
    read = jnp.transpose(read_ref[...])

    def mix(layer):
        return jnp.dot(msg[layer], hidden_ref[...], preferred_element_type=F32).astype(BF16)

    mixed = mix(0)

    place = pos_ref[0:4, :]
    pieces = split(place)
    norm = norm_of(place)
    right_rows(rows_ref, pieces, norm)
    near_ref[...] = rows_ref[...].astype(BF16)
    left_rows(rows_ref, pieces, norm)
    for b in range(tiles):
        at = slice(128 * b, 128 * (b + 1))
        mine_ref[at, :] = jnp.transpose(rows_ref[:, at]).astype(BF16)
    for g, value in enumerate(pieces):
        rows_ref[4 * g : 4 * g + 4, :] = value
    rows_ref[3:4, :] = jnp.ones((1, size), F32)
    rows_ref[12:16, :] = jnp.zeros((4, size), F32)
    side_ref[...] = rows_ref[0:16, :].astype(BF16)
    square_ref[...] = jnp.dot(mine_ref[...], near_ref[...], preferred_element_type=F32)

    index = low_ref[...]
    low_ref[...] = index & 127
    unit_ref[...] = jnp.int32(1) << ((index >> 7) << 3)
    rows = lax.broadcasted_iota(jnp.int32, (128, 128), 0)

    def count(b):
        lanes = slice(128 * b, 128 * (b + 1))
        total = jnp.zeros((128, 128), jnp.int32)
        for k in range(neighbours):
            total += jnp.where(rows == low_ref[k : k + 1, lanes], unit_ref[k : k + 1, lanes], 0)
        count_ref[:, lanes] = total

    step = 32
    limit = RADIUS * RADIUS
    per_basis = 4.0 * RADIUS / basis_count / math.log(2.0)
    series = [value / limit ** (k + 1) for k, value in enumerate(COSINE)]

    def pairs(lanes):
        for s in range(size // step):
            here = slice(step * s, step * (s + 1))
            f, first = divmod(step * s, 128)
            times = ((count_ref[first : first + step, lanes] >> (8 * f)) & 255).astype(F32)
            near = jnp.minimum(square_ref[here, lanes], limit)
            root = series[-1]
            for value in series[-2::-1]:
                root = root * near + value
            root = (limit - near) * root
            envelope = root * root * times
            pull_ref[here, lanes] = envelope
            growth = jnp.exp2(near * lax.rsqrt(near) * per_basis)
            basis = jnp.exp2(near * (-2.0 / math.log(2.0))) * envelope
            for n in range(basis_count):
                basis_ref[n, here, lanes] = basis.astype(BF16)
                if n + 1 < basis_count:
                    basis = basis * growth

    number = lax.broadcasted_iota(jnp.int32, (basis_count, channels), 0).astype(F32)
    center = number * (RADIUS / basis_count)
    scale = jnp.exp(center * center * -2.0) * (1.0 / math.sqrt(neighbours))
    radial = [jnp.transpose(radial_ref[layer] * scale) for layer in range(layers)]

    def advance(layer, lanes, mixed):
        message = 0.0
        for n in range(basis_count):
            message += radial[layer][:, n : n + 1] * jnp.dot(
                mixed, basis_ref[n, :, lanes], preferred_element_type=F32
            )
        active = jax.nn.silu(message).astype(BF16)
        change = jnp.dot(out_w[layer], active, preferred_element_type=F32)
        return (hidden_ref[:, lanes].astype(F32) + change).astype(BF16)

    parts = [slice(own * part, own * (part + 1)) for part in range(HALVES)]
    for part, lanes in enumerate(parts):
        for b in range(tiles // HALVES):
            count(tiles // HALVES * part + b)
        pairs(lanes)
    for layer in range(layers):
        if layer > 0:
            mixed = mix(layer)
        later = [advance(layer, lanes, mixed) for lanes in parts]
        for lanes, value in zip(parts, later):
            hidden_ref[:, lanes] = value

    half = lax.axis_index("ml") // (sources // HALVES)
    mine = pl.ds(pl.multiple_of(half * own, own), own)
    key = jnp.transpose(
        jnp.dot(read[channels:], hidden_ref[...], preferred_element_type=F32)
    ).astype(BF16)
    query = jnp.dot(read[:channels], hidden_ref[:, mine], preferred_element_type=F32).astype(BF16)
    side = side_ref[...]
    total = jnp.zeros((16, own), F32)
    for here in parts:
        pull = jnp.dot(key[here], query, preferred_element_type=F32) * (
            pull_ref[here, mine] * (1.0 / channels)
        )
        high = pull.astype(BF16)
        rest = (pull - high.astype(F32)).astype(BF16)
        total += jnp.dot(side[:, here], high, preferred_element_type=F32)
        total += jnp.dot(side[:, here], rest, preferred_element_type=F32)
    sums = total[0:4] + total[4:8] + total[8:12]
    force = sums[0:3] - pos_ref[0:3, mine] * sums[3:4]
    force_ref[...] = jnp.zeros_like(force_ref)
    for place, a in enumerate(exchange_order(own // share)):
        force_ref[place, 0:3, 0:share] = force[:, share * a : share * (a + 1)]


def pair_kernel(
    tiles_hbm_ref,
    own_ref,
    low_ref,
    high_ref,
    force_ref,
    rows_ref,
    value_ref,
    near_ref,
    side_ref,
    mine_ref,
    tiles_ref,
    tiles_sem,
):
    listed, tiles = tiles_ref.shape
    tiles_copy = pltpu.make_async_copy(tiles_hbm_ref, tiles_ref, tiles_sem)
    tiles_copy.start()
    for which, ref in enumerate((low_ref, own_ref, high_ref)):
        place = ref[...]
        pieces = split(place)
        norm = norm_of(place)
        right_rows(rows_ref, pieces, norm)
        charge = place[3:4]
        weighted = jnp.concatenate([place[0:3] * charge, charge], axis=0)
        for g, value in enumerate(split(weighted)):
            value_ref[4 * g : 4 * g + 4, :] = value
        value_ref[12:16, :] = jnp.zeros_like(place)
        for t in range(tiles):
            lanes = slice(TILE * t, TILE * (t + 1))
            near_ref[which * tiles + t] = rows_ref[:, lanes].astype(BF16)
            side_ref[which * tiles + t] = value_ref[:, lanes].astype(BF16)
    place = own_ref[...]
    is_place = lax.broadcasted_iota(jnp.int32, place.shape, 0) < 3
    left_rows(rows_ref, [jnp.where(is_place, piece, 0.0) for piece in split(place)], norm_of(place))
    for t in range(tiles):
        lanes = slice(TILE * t, TILE * (t + 1))
        mine_ref[lanes, :] = jnp.transpose(rows_ref[:, lanes]).astype(BF16)
    across = (((1,), (1,)), ((), ()))
    tiles_copy.wait()
    for t in range(tiles):
        lanes = slice(TILE * t, TILE * (t + 1))
        mine = mine_ref[lanes, :]
        total = jnp.zeros((TILE, 16), F32)
        for c in range(0, listed, 2):
            first, second = tiles_ref[c, t], tiles_ref[c + 1, t]
            squared = jnp.dot(
                mine,
                jnp.concatenate([near_ref[first], near_ref[second]], axis=1),
                preferred_element_type=F32,
            )
            inverse = lax.rsqrt(squared)
            total += lax.dot_general(
                (inverse * inverse * inverse).astype(BF16),
                jnp.concatenate([side_ref[first], side_ref[second]], axis=1),
                across,
                preferred_element_type=F32,
            )
        turned = jnp.transpose(total)
        sums = turned[0:4] + turned[4:8] + turned[8:12]
        place = own_ref[:, lanes]
        force_ref[:, lanes] = (place[0:3] * sums[3:4] - sums[0:3]) * (place[3:4] * COULOMB)


def vmem(count):
    return [pl.BlockSpec(memory_space=pltpu.VMEM)] * count


def on_device(
    mm_positions,
    mm_charge,
    mm_tiles,
    ml_feat,
    ml_positions,
    ml_neighbours,
    msg_weight,
    radial_weight,
    out_weight,
    read_weight,
):
    patches, share, channels = ml_feat.shape
    atom_count = mm_positions.shape[1]
    tile_count, listed = mm_tiles.shape
    members = lax.axis_size("ml")
    size = members * share
    own = size // HALVES
    neighbours = ml_neighbours.shape[1]
    basis_count = radial_weight.shape[1]
    limit = 48 * 1024 * 1024

    send, atoms, near_radial = pl.pallas_call(
        pack_kernel,
        out_shape=(
            jax.ShapeDtypeStruct((members, share + 16, channels), BF16),
            pltpu.VMEM((4, atom_count), F32),
            pltpu.VMEM(radial_weight.shape, F32),
        ),
        in_specs=vmem(6),
        out_specs=tuple(vmem(3)),
        scratch_shapes=[pltpu.VMEM((patches, 16, 128), F32)],
        cost_estimate=pl.CostEstimate(flops=1000, bytes_accessed=400000, transcendentals=0),
    )(
        ml_feat,
        ml_positions.transpose(1, 0, 2),
        ml_neighbours,
        mm_positions,
        mm_charge.reshape(1, atom_count),
        radial_weight,
    )
    recv = lax.all_to_all(
        send,
        "ml",
        split_axis=0,
        concat_axis=0,
        tiled=True,
        axis_index_groups=[exchange_order(members)],
    )

    devices = lax.axis_size(("dom", "ml"))
    forward = [(i, (i + 1) % devices) for i in range(devices)]
    backward = [(b, a) for a, b in forward]
    low = lax.ppermute(atoms, ("dom", "ml"), forward)
    high = lax.ppermute(atoms, ("dom", "ml"), backward)

    forces = pl.pallas_call(
        patch_kernel,
        out_shape=jax.ShapeDtypeStruct((own // share, 8, 128), F32),
        in_specs=vmem(5),
        out_specs=vmem(1)[0],
        scratch_shapes=[
            pltpu.VMEM((size, channels), BF16),
            pltpu.VMEM((channels, size), BF16),
            pltpu.VMEM((8, size), F32),
            pltpu.VMEM((32, size), F32),
            pltpu.VMEM((32, size), BF16),
            pltpu.VMEM((size, 32), BF16),
            pltpu.VMEM((16, size), BF16),
            pltpu.VMEM((neighbours, size), jnp.int32),
            pltpu.VMEM((neighbours, size), jnp.int32),
            pltpu.VMEM((128, size), jnp.int32),
            pltpu.VMEM((size, size), F32),
            pltpu.VMEM((basis_count, size, size), BF16),
            pltpu.VMEM((size, size), F32),
        ],
        compiler_params=pltpu.CompilerParams(vmem_limit_bytes=limit),
        cost_estimate=pl.CostEstimate(
            flops=5 * 10**9, bytes_accessed=1000000, transcendentals=10**6
        ),
    )(recv, msg_weight, near_radial, out_weight, read_weight)
    groups = [[h * patches + p for p in exchange_order(patches)] for h in range(HALVES)]
    returned = lax.all_to_all(
        forces, "ml", split_axis=0, concat_axis=0, tiled=True, axis_index_groups=groups
    )
    ml_force = returned[:, :3, :share]

    mm_force = pl.pallas_call(
        pair_kernel,
        out_shape=jax.ShapeDtypeStruct((3, atom_count), F32),
        in_specs=[pl.BlockSpec(memory_space=pl.ANY)] + vmem(3),
        out_specs=vmem(1)[0],
        scratch_shapes=[
            pltpu.VMEM((32, atom_count), F32),
            pltpu.VMEM((16, atom_count), F32),
            pltpu.VMEM((3 * tile_count, 32, TILE), BF16),
            pltpu.VMEM((3 * tile_count, 16, TILE), BF16),
            pltpu.VMEM((atom_count, 32), BF16),
            pltpu.SMEM((listed, tile_count), jnp.int32),
            pltpu.SemaphoreType.DMA,
        ],
        compiler_params=pltpu.CompilerParams(vmem_limit_bytes=limit),
        cost_estimate=pl.CostEstimate(
            flops=4 * 10**9, bytes_accessed=200000, transcendentals=10**6
        ),
    )(mm_tiles.T, atoms, low, high)
    return (mm_force, ml_force)


def solution(mesh):
    in_specs = (
        P(None, ("dom", "ml")),
        P(("dom", "ml")),
        P(("dom", "ml"), None),
        P("dom", "ml", None),
        P("dom", None, "ml"),
        P("dom", None, "ml"),
        P(),
        P(),
        P(),
        P(),
    )
    out_specs = (P(None, ("dom", "ml")), P("dom", None, "ml"))
    return jax.shard_map(
        on_device, mesh=mesh, in_specs=in_specs, out_specs=out_specs, check_vma=False
    )
```

```python
import math

import jax
import jax.numpy as jnp
from jax import lax
from jax.experimental import pallas as pl
from jax.experimental.pallas import tpu as pltpu
from jax.sharding import PartitionSpec as P

TILE = 128
RADIUS = 6.0
SOFTEN = 1.0
COULOMB = 0.5
HALVES = 2
FIELDS = 5
BITS = 6


FIRST = {16: 10, 8: 2}


def exchange_order(count):
    first = FIRST.get(count, count - 1)
    return [first] + [member for member in range(count)[::-1] if member != first]


COSINE = (
    0.9999999991255941,
    -0.23370050635000697,
    0.019968606683524803,
    -0.0008935362638784474,
    2.3601070666008123e-05,
)

F32 = jnp.float32
BF16 = jnp.bfloat16


def split(value):
    high = value.astype(BF16).astype(F32)
    rest = value - high
    middle = rest.astype(BF16).astype(F32)
    return high, middle, rest - middle


LEFT = (0, 0, 1, 1, 0, 2)
RIGHT = (0, 1, 0, 1, 2, 0)


def left_rows(rows_ref, pieces, norm):
    for g, which in enumerate(LEFT):
        rows_ref[4 * g : 4 * g + 4, :] = pieces[which]
    for g, value in enumerate(split(norm + SOFTEN)):
        rows_ref[24 + g : 25 + g, :] = value
    rows_ref[27:30, :] = jnp.ones((3, norm.shape[1]), F32)
    rows_ref[30:32, :] = jnp.zeros((2, norm.shape[1]), F32)


def right_rows(rows_ref, pieces, norm):
    for g, which in enumerate(RIGHT):
        rows_ref[4 * g : 4 * g + 4, :] = pieces[which] * -2.0
    rows_ref[24:27, :] = jnp.ones((3, norm.shape[1]), F32)
    for g, value in enumerate(split(norm)):
        rows_ref[27 + g : 28 + g, :] = value
    rows_ref[30:32, :] = jnp.zeros((2, norm.shape[1]), F32)


def norm_of(place):
    return place[0:1] * place[0:1] + place[1:2] * place[1:2] + place[2:3] * place[2:3]


def pack_kernel(
    feat_ref,
    pos_ref,
    nb_ref,
    mm_pos_ref,
    mm_charge_ref,
    radial_ref,
    send_ref,
    atoms_ref,
    near_radial_ref,
    geo_ref,
):
    patches, atoms, _ = feat_ref.shape
    members = send_ref.shape[0]
    holder = exchange_order(patches)
    geo_ref[...] = jnp.zeros_like(geo_ref)
    high, middle, low = split(pos_ref[...])
    for p in range(patches):
        numbers = (nb_ref[p] - 256).astype(F32)
        geo_ref[p, 0:16, 0:32] = numbers[0:16]
        geo_ref[p, 0:16, 32:64] = numbers[16:32]
        for axis in range(3):
            geo_ref[p, axis : axis + 1, 64:96] = high[axis, p : p + 1]
            geo_ref[p, axis : axis + 1, 96:128] = middle[axis, p : p + 1]
            geo_ref[p, axis + 8 : axis + 9, 64:96] = low[axis, p : p + 1]
        block = geo_ref[p].astype(BF16)
        for place, member in enumerate(exchange_order(members)):
            if member % patches == holder[p]:
                send_ref[place, 0:atoms, :] = feat_ref[p]
                send_ref[place, atoms : atoms + 16, :] = block
    atoms_ref[0:3, :] = mm_pos_ref[...]
    atoms_ref[3:4, :] = mm_charge_ref[...]
    near_radial_ref[...] = radial_ref[...]


def patch_kernel(
    recv_ref,
    msg_ref,
    radial_ref,
    out_w_ref,
    read_ref,
    force_ref,
    plain_ref,
    hidden_ref,
    pos_ref,
    rows_ref,
    near_ref,
    mine_ref,
    side_ref,
    low_ref,
    unit_ref,
    count_ref,
    square_ref,
    basis_ref,
    pull_ref,
):
    sources = recv_ref.shape[0]
    share = recv_ref.shape[1] - 16
    size = sources * share
    own = size // HALVES
    neighbours = low_ref.shape[0]
    basis_count = radial_ref.shape[1]
    layers = msg_ref.shape[0]
    channels = recv_ref.shape[2]
    tiles = size // 128

    for place, m in enumerate(exchange_order(sources)):
        plain_ref[share * m : share * (m + 1), :] = recv_ref[place, 0:share, :]
        geo = recv_ref[place, share : share + 16, :].astype(F32)
        lanes = slice(share * m, share * (m + 1))
        pos_ref[:, lanes] = (geo[0:8, 64:96] + geo[0:8, 96:128]) + geo[8:16, 64:96]
        low_ref[0:16, lanes] = geo[:, 0:32].astype(jnp.int32) + 256
        low_ref[16:32, lanes] = geo[:, 32:64].astype(jnp.int32) + 256
    hidden_ref[...] = jnp.transpose(plain_ref[...])
    msg = [jnp.transpose(msg_ref[layer]) for layer in range(layers)]
    out_w = [jnp.transpose(out_w_ref[layer]) for layer in range(layers)]
    read = jnp.transpose(read_ref[...])

    def mix(layer):
        return jnp.dot(msg[layer], hidden_ref[...], preferred_element_type=F32).astype(BF16)

    mixed = mix(0)

    place = pos_ref[0:4, :]
    pieces = split(place)
    norm = norm_of(place)
    right_rows(rows_ref, pieces, norm)
    near_ref[...] = rows_ref[...].astype(BF16)
    left_rows(rows_ref, pieces, norm)
    for b in range(tiles):
        at = slice(128 * b, 128 * (b + 1))
        mine_ref[at, :] = jnp.transpose(rows_ref[:, at]).astype(BF16)
    for g, value in enumerate(pieces):
        rows_ref[4 * g : 4 * g + 4, :] = value
    rows_ref[3:4, :] = jnp.ones((1, size), F32)
    rows_ref[12:16, :] = jnp.zeros((4, size), F32)
    side_ref[...] = rows_ref[0:16, :].astype(BF16)
    square_ref[...] = jnp.dot(mine_ref[...], near_ref[...], preferred_element_type=F32)

    index = low_ref[...]
    depth = count_ref.shape[0]
    field = jnp.zeros_like(index)
    for f in range(1, FIELDS):
        field += (index >= depth * f).astype(jnp.int32)
    low_ref[...] = index - field * depth
    unit_ref[...] = jnp.int32(1) << (field * BITS)
    rows = lax.broadcasted_iota(jnp.int32, (depth, 128), 0)

    def count(b):
        lanes = slice(128 * b, 128 * (b + 1))
        total = jnp.zeros((depth, 128), jnp.int32)
        for k in range(neighbours):
            total += jnp.where(rows == low_ref[k : k + 1, lanes], unit_ref[k : k + 1, lanes], 0)
        count_ref[:, lanes] = total

    step = 32
    limit = RADIUS * RADIUS
    per_basis = 4.0 * RADIUS / basis_count / math.log(2.0)
    series = [value / limit ** (k + 1) for k, value in enumerate(COSINE)]

    def pairs(lanes):
        for s in range(size // step):
            here = slice(step * s, step * (s + 1))
            found = []
            for group in range(0, step, 8):
                f, first = divmod(step * s + group, depth)
                packed = count_ref[first : first + 8, lanes]
                found.append((packed >> (BITS * f)) & ((1 << BITS) - 1))
            times = jnp.concatenate(found, axis=0).astype(F32)
            near = jnp.minimum(square_ref[here, lanes], limit)
            root = series[-1]
            for value in series[-2::-1]:
                root = root * near + value
            root = (limit - near) * root
            envelope = root * root * times
            pull_ref[here, lanes] = envelope
            growth = jnp.exp2(near * lax.rsqrt(near) * per_basis)
            basis = jnp.exp2(near * (-2.0 / math.log(2.0))) * envelope
            for n in range(basis_count):
                basis_ref[n, here, lanes] = basis.astype(BF16)
                if n + 1 < basis_count:
                    basis = basis * growth

    number = lax.broadcasted_iota(jnp.int32, (basis_count, channels), 0).astype(F32)
    center = number * (RADIUS / basis_count)
    scale = jnp.exp(center * center * -2.0) * (1.0 / math.sqrt(neighbours))
    radial = [jnp.transpose(radial_ref[layer] * scale) for layer in range(layers)]

    def advance(layer, lanes, mixed):
        message = 0.0
        for n in range(basis_count):
            message += radial[layer][:, n : n + 1] * jnp.dot(
                mixed, basis_ref[n, :, lanes], preferred_element_type=F32
            )
        active = jax.nn.silu(message).astype(BF16)
        change = jnp.dot(out_w[layer], active, preferred_element_type=F32)
        return (hidden_ref[:, lanes].astype(F32) + change).astype(BF16)

    parts = [slice(own * part, own * (part + 1)) for part in range(HALVES)]
    for part, lanes in enumerate(parts):
        for b in range(tiles // HALVES):
            count(tiles // HALVES * part + b)
        pairs(lanes)
    for layer in range(layers):
        if layer > 0:
            mixed = mix(layer)
        later = [advance(layer, lanes, mixed) for lanes in parts]
        for lanes, value in zip(parts, later):
            hidden_ref[:, lanes] = value

    half = lax.axis_index("ml") // (sources // HALVES)
    mine = pl.ds(pl.multiple_of(half * own, own), own)
    key = jnp.transpose(
        jnp.dot(read[channels:], hidden_ref[...], preferred_element_type=F32)
    ).astype(BF16)
    query = jnp.dot(read[:channels], hidden_ref[:, mine], preferred_element_type=F32).astype(BF16)
    side = side_ref[...]
    total = jnp.zeros((16, own), F32)
    for here in parts:
        pull = jnp.dot(key[here], query, preferred_element_type=F32) * (
            pull_ref[here, mine] * (1.0 / channels)
        )
        high = pull.astype(BF16)
        rest = (pull - high.astype(F32)).astype(BF16)
        total += jnp.dot(side[:, here], high, preferred_element_type=F32)
        total += jnp.dot(side[:, here], rest, preferred_element_type=F32)
    sums = total[0:4] + total[4:8] + total[8:12]
    force = sums[0:3] - pos_ref[0:3, mine] * sums[3:4]
    force_ref[...] = jnp.zeros_like(force_ref)
    for place, a in enumerate(exchange_order(own // share)):
        force_ref[place, 0:3, 0:share] = force[:, share * a : share * (a + 1)]


def pair_kernel(
    tiles_hbm_ref,
    own_ref,
    low_ref,
    high_ref,
    force_ref,
    rows_ref,
    value_ref,
    near_ref,
    side_ref,
    mine_ref,
    tiles_ref,
    tiles_sem,
):
    listed, tiles = tiles_ref.shape
    tiles_copy = pltpu.make_async_copy(tiles_hbm_ref, tiles_ref, tiles_sem)
    tiles_copy.start()
    for which, ref in enumerate((low_ref, own_ref, high_ref)):
        place = ref[...]
        pieces = split(place)
        norm = norm_of(place)
        right_rows(rows_ref, pieces, norm)
        charge = place[3:4]
        weighted = jnp.concatenate([place[0:3] * charge, charge], axis=0)
        for g, value in enumerate(split(weighted)):
            value_ref[4 * g : 4 * g + 4, :] = value
        value_ref[12:16, :] = jnp.zeros_like(place)
        for t in range(tiles):
            lanes = slice(TILE * t, TILE * (t + 1))
            near_ref[which * tiles + t] = rows_ref[:, lanes].astype(BF16)
            side_ref[which * tiles + t] = value_ref[:, lanes].astype(BF16)
    place = own_ref[...]
    is_place = lax.broadcasted_iota(jnp.int32, place.shape, 0) < 3
    left_rows(rows_ref, [jnp.where(is_place, piece, 0.0) for piece in split(place)], norm_of(place))
    for t in range(tiles):
        lanes = slice(TILE * t, TILE * (t + 1))
        mine_ref[lanes, :] = jnp.transpose(rows_ref[:, lanes]).astype(BF16)
    across = (((1,), (1,)), ((), ()))
    tiles_copy.wait()
    for t in range(tiles):
        lanes = slice(TILE * t, TILE * (t + 1))
        mine = mine_ref[lanes, :]
        total = jnp.zeros((TILE, 16), F32)
        for c in range(0, listed, 2):
            first, second = tiles_ref[c, t], tiles_ref[c + 1, t]
            squared = jnp.dot(
                mine,
                jnp.concatenate([near_ref[first], near_ref[second]], axis=1),
                preferred_element_type=F32,
            )
            inverse = lax.rsqrt(squared)
            total += lax.dot_general(
                (inverse * inverse * inverse).astype(BF16),
                jnp.concatenate([side_ref[first], side_ref[second]], axis=1),
                across,
                preferred_element_type=F32,
            )
        turned = jnp.transpose(total)
        sums = turned[0:4] + turned[4:8] + turned[8:12]
        place = own_ref[:, lanes]
        force_ref[:, lanes] = (place[0:3] * sums[3:4] - sums[0:3]) * (place[3:4] * COULOMB)


def vmem(count):
    return [pl.BlockSpec(memory_space=pltpu.VMEM)] * count


def on_device(
    mm_positions,
    mm_charge,
    mm_tiles,
    ml_feat,
    ml_positions,
    ml_neighbours,
    msg_weight,
    radial_weight,
    out_weight,
    read_weight,
):
    patches, share, channels = ml_feat.shape
    atom_count = mm_positions.shape[1]
    tile_count, listed = mm_tiles.shape
    members = lax.axis_size("ml")
    size = members * share
    own = size // HALVES
    neighbours = ml_neighbours.shape[1]
    basis_count = radial_weight.shape[1]
    limit = 48 * 1024 * 1024

    send, atoms, near_radial = pl.pallas_call(
        pack_kernel,
        out_shape=(
            jax.ShapeDtypeStruct((members, share + 16, channels), BF16),
            pltpu.VMEM((4, atom_count), F32),
            pltpu.VMEM(radial_weight.shape, F32),
        ),
        in_specs=vmem(6),
        out_specs=tuple(vmem(3)),
        scratch_shapes=[pltpu.VMEM((patches, 16, 128), F32)],
        cost_estimate=pl.CostEstimate(flops=1000, bytes_accessed=400000, transcendentals=0),
    )(
        ml_feat,
        ml_positions.transpose(1, 0, 2),
        ml_neighbours,
        mm_positions,
        mm_charge.reshape(1, atom_count),
        radial_weight,
    )
    recv = lax.all_to_all(
        send,
        "ml",
        split_axis=0,
        concat_axis=0,
        tiled=True,
        axis_index_groups=[exchange_order(members)],
    )

    devices = lax.axis_size(("dom", "ml"))
    forward = [(i, (i + 1) % devices) for i in range(devices)]
    backward = [(b, a) for a, b in forward]
    low = lax.ppermute(atoms, ("dom", "ml"), forward)
    high = lax.ppermute(atoms, ("dom", "ml"), backward)

    forces = pl.pallas_call(
        patch_kernel,
        out_shape=jax.ShapeDtypeStruct((own // share, 8, 128), F32),
        in_specs=vmem(5),
        out_specs=vmem(1)[0],
        scratch_shapes=[
            pltpu.VMEM((size, channels), BF16),
            pltpu.VMEM((channels, size), BF16),
            pltpu.VMEM((8, size), F32),
            pltpu.VMEM((32, size), F32),
            pltpu.VMEM((32, size), BF16),
            pltpu.VMEM((size, 32), BF16),
            pltpu.VMEM((16, size), BF16),
            pltpu.VMEM((neighbours, size), jnp.int32),
            pltpu.VMEM((neighbours, size), jnp.int32),
            pltpu.VMEM((-(-size // (8 * FIELDS)) * 8, size), jnp.int32),
            pltpu.VMEM((size, size), F32),
            pltpu.VMEM((basis_count, size, size), BF16),
            pltpu.VMEM((size, size), F32),
        ],
        compiler_params=pltpu.CompilerParams(vmem_limit_bytes=limit),
        cost_estimate=pl.CostEstimate(
            flops=5 * 10**9, bytes_accessed=1000000, transcendentals=10**6
        ),
    )(recv, msg_weight, near_radial, out_weight, read_weight)
    groups = [[h * patches + p for p in exchange_order(patches)] for h in range(HALVES)]
    returned = lax.all_to_all(
        forces, "ml", split_axis=0, concat_axis=0, tiled=True, axis_index_groups=groups
    )
    ml_force = returned[:, :3, :share]

    mm_force = pl.pallas_call(
        pair_kernel,
        out_shape=jax.ShapeDtypeStruct((3, atom_count), F32),
        in_specs=[pl.BlockSpec(memory_space=pl.ANY)] + vmem(3),
        out_specs=vmem(1)[0],
        scratch_shapes=[
            pltpu.VMEM((32, atom_count), F32),
            pltpu.VMEM((16, atom_count), F32),
            pltpu.VMEM((3 * tile_count, 32, TILE), BF16),
            pltpu.VMEM((3 * tile_count, 16, TILE), BF16),
            pltpu.VMEM((atom_count, 32), BF16),
            pltpu.SMEM((listed, tile_count), jnp.int32),
            pltpu.SemaphoreType.DMA,
        ],
        compiler_params=pltpu.CompilerParams(vmem_limit_bytes=limit),
        cost_estimate=pl.CostEstimate(
            flops=4 * 10**9, bytes_accessed=200000, transcendentals=10**6
        ),
    )(mm_tiles.T, atoms, low, high)
    return (mm_force, ml_force)


def solution(mesh):
    in_specs = (
        P(None, ("dom", "ml")),
        P(("dom", "ml")),
        P(("dom", "ml"), None),
        P("dom", "ml", None),
        P("dom", None, "ml"),
        P("dom", None, "ml"),
        P(),
        P(),
        P(),
        P(),
    )
    out_specs = (P(None, ("dom", "ml")), P("dom", None, "ml"))
    return jax.shard_map(
        on_device, mesh=mesh, in_specs=in_specs, out_specs=out_specs, check_vma=False
    )
```

```python
import math

import jax
import jax.numpy as jnp
from jax import lax
from jax.experimental import pallas as pl
from jax.experimental.pallas import tpu as pltpu
from jax.sharding import PartitionSpec as P

TILE = 128
RADIUS = 6.0
SOFTEN = 1.0
COULOMB = 0.5
HALVES = 2
FIELDS = 5
BITS = 6


FIRST = {16: 11, 8: 2}


def exchange_order(count):
    first = FIRST.get(count, count - 1)
    return [first] + [member for member in range(count)[::-1] if member != first]


COSINE = (
    0.9999999991255941,
    -0.23370050635000697,
    0.019968606683524803,
    -0.0008935362638784474,
    2.3601070666008123e-05,
)

F32 = jnp.float32
BF16 = jnp.bfloat16


def split(value):
    high = value.astype(BF16).astype(F32)
    rest = value - high
    middle = rest.astype(BF16).astype(F32)
    return high, middle, rest - middle


LEFT = (0, 0, 1, 1, 0, 2)
RIGHT = (0, 1, 0, 1, 2, 0)


def left_rows(rows_ref, pieces, norm):
    for g, which in enumerate(LEFT):
        rows_ref[4 * g : 4 * g + 4, :] = pieces[which]
    for g, value in enumerate(split(norm + SOFTEN)):
        rows_ref[24 + g : 25 + g, :] = value
    rows_ref[27:30, :] = jnp.ones((3, norm.shape[1]), F32)
    rows_ref[30:32, :] = jnp.zeros((2, norm.shape[1]), F32)


def right_rows(rows_ref, pieces, norm):
    for g, which in enumerate(RIGHT):
        rows_ref[4 * g : 4 * g + 4, :] = pieces[which] * -2.0
    rows_ref[24:27, :] = jnp.ones((3, norm.shape[1]), F32)
    for g, value in enumerate(split(norm)):
        rows_ref[27 + g : 28 + g, :] = value
    rows_ref[30:32, :] = jnp.zeros((2, norm.shape[1]), F32)


def norm_of(place):
    return place[0:1] * place[0:1] + place[1:2] * place[1:2] + place[2:3] * place[2:3]


def pack_kernel(
    feat_ref,
    pos_ref,
    nb_ref,
    mm_pos_ref,
    mm_charge_ref,
    radial_ref,
    send_ref,
    atoms_ref,
    near_radial_ref,
    geo_ref,
):
    patches, atoms, _ = feat_ref.shape
    members = send_ref.shape[0]
    holder = exchange_order(patches)
    geo_ref[...] = jnp.zeros_like(geo_ref)
    high, middle, low = split(pos_ref[...])
    for p in range(patches):
        numbers = (nb_ref[p] - 256).astype(F32)
        geo_ref[p, 0:16, 0:32] = numbers[0:16]
        geo_ref[p, 0:16, 32:64] = numbers[16:32]
        for axis in range(3):
            geo_ref[p, axis : axis + 1, 64:96] = high[axis, p : p + 1]
            geo_ref[p, axis : axis + 1, 96:128] = middle[axis, p : p + 1]
            geo_ref[p, axis + 8 : axis + 9, 64:96] = low[axis, p : p + 1]
        block = geo_ref[p].astype(BF16)
        for place, member in enumerate(exchange_order(members)):
            if member % patches == holder[p]:
                send_ref[place, 0:atoms, :] = feat_ref[p]
                send_ref[place, atoms : atoms + 16, :] = block
    atoms_ref[0:3, :] = mm_pos_ref[...]
    atoms_ref[3:4, :] = mm_charge_ref[...]
    near_radial_ref[...] = radial_ref[...]


def patch_kernel(
    recv_ref,
    msg_ref,
    radial_ref,
    out_w_ref,
    read_ref,
    force_ref,
    plain_ref,
    hidden_ref,
    pos_ref,
    rows_ref,
    near_ref,
    mine_ref,
    side_ref,
    low_ref,
    unit_ref,
    count_ref,
    square_ref,
    basis_ref,
    pull_ref,
):
    sources = recv_ref.shape[0]
    share = recv_ref.shape[1] - 16
    size = sources * share
    own = size // HALVES
    neighbours = low_ref.shape[0]
    basis_count = radial_ref.shape[1]
    layers = msg_ref.shape[0]
    channels = recv_ref.shape[2]
    tiles = size // 128

    for place, m in enumerate(exchange_order(sources)):
        plain_ref[share * m : share * (m + 1), :] = recv_ref[place, 0:share, :]
        geo = recv_ref[place, share : share + 16, :].astype(F32)
        lanes = slice(share * m, share * (m + 1))
        pos_ref[:, lanes] = (geo[0:8, 64:96] + geo[0:8, 96:128]) + geo[8:16, 64:96]
        low_ref[0:16, lanes] = geo[:, 0:32].astype(jnp.int32) + 256
        low_ref[16:32, lanes] = geo[:, 32:64].astype(jnp.int32) + 256
    hidden_ref[...] = jnp.transpose(plain_ref[...])
    msg = [jnp.transpose(msg_ref[layer]) for layer in range(layers)]
    out_w = [jnp.transpose(out_w_ref[layer]) for layer in range(layers)]
    read = jnp.transpose(read_ref[...])

    def mix(layer):
        return jnp.dot(msg[layer], hidden_ref[...], preferred_element_type=F32).astype(BF16)

    mixed = mix(0)

    place = pos_ref[0:4, :]
    pieces = split(place)
    norm = norm_of(place)
    right_rows(rows_ref, pieces, norm)
    near_ref[...] = rows_ref[...].astype(BF16)
    left_rows(rows_ref, pieces, norm)
    for b in range(tiles):
        at = slice(128 * b, 128 * (b + 1))
        mine_ref[at, :] = jnp.transpose(rows_ref[:, at]).astype(BF16)
    for g, value in enumerate(pieces):
        rows_ref[4 * g : 4 * g + 4, :] = value
    rows_ref[3:4, :] = jnp.ones((1, size), F32)
    rows_ref[12:16, :] = jnp.zeros((4, size), F32)
    side_ref[...] = rows_ref[0:16, :].astype(BF16)
    square_ref[...] = jnp.dot(mine_ref[...], near_ref[...], preferred_element_type=F32)

    index = low_ref[...]
    depth = count_ref.shape[0]
    field = jnp.zeros_like(index)
    for f in range(1, FIELDS):
        field += (index >= depth * f).astype(jnp.int32)
    low_ref[...] = index - field * depth
    unit_ref[...] = jnp.int32(1) << (field * BITS)
    rows = lax.broadcasted_iota(jnp.int32, (depth, 128), 0)

    def count(b):
        lanes = slice(128 * b, 128 * (b + 1))
        total = jnp.zeros((depth, 128), jnp.int32)
        for k in range(neighbours):
            total += jnp.where(rows == low_ref[k : k + 1, lanes], unit_ref[k : k + 1, lanes], 0)
        count_ref[:, lanes] = total

    step = 32
    limit = RADIUS * RADIUS
    per_basis = 4.0 * RADIUS / basis_count / math.log(2.0)
    series = [value / limit ** (k + 1) for k, value in enumerate(COSINE)]

    def pairs(lanes):
        for s in range(size // step):
            here = slice(step * s, step * (s + 1))
            found = []
            for group in range(0, step, 8):
                f, first = divmod(step * s + group, depth)
                packed = count_ref[first : first + 8, lanes]
                found.append((packed >> (BITS * f)) & ((1 << BITS) - 1))
            times = jnp.concatenate(found, axis=0).astype(F32)
            near = jnp.minimum(square_ref[here, lanes], limit)
            root = series[-1]
            for value in series[-2::-1]:
                root = root * near + value
            root = (limit - near) * root
            envelope = root * root * times
            pull_ref[here, lanes] = envelope
            growth = jnp.exp2(near * lax.rsqrt(near) * per_basis)
            basis = jnp.exp2(near * (-2.0 / math.log(2.0))) * envelope
            for n in range(basis_count):
                basis_ref[n, here, lanes] = basis.astype(BF16)
                if n + 1 < basis_count:
                    basis = basis * growth

    number = lax.broadcasted_iota(jnp.int32, (basis_count, channels), 0).astype(F32)
    center = number * (RADIUS / basis_count)
    scale = jnp.exp(center * center * -2.0) * (1.0 / math.sqrt(neighbours))
    radial = [jnp.transpose(radial_ref[layer] * scale) for layer in range(layers)]

    def advance(layer, lanes, mixed):
        message = 0.0
        for n in range(basis_count):
            message += radial[layer][:, n : n + 1] * jnp.dot(
                mixed, basis_ref[n, :, lanes], preferred_element_type=F32
            )
        active = jax.nn.silu(message).astype(BF16)
        change = jnp.dot(out_w[layer], active, preferred_element_type=F32)
        return (hidden_ref[:, lanes].astype(F32) + change).astype(BF16)

    parts = [slice(own * part, own * (part + 1)) for part in range(HALVES)]
    for part, lanes in enumerate(parts):
        for b in range(tiles // HALVES):
            count(tiles // HALVES * part + b)
        pairs(lanes)
    for layer in range(layers):
        if layer > 0:
            mixed = mix(layer)
        later = [advance(layer, lanes, mixed) for lanes in parts]
        for lanes, value in zip(parts, later):
            hidden_ref[:, lanes] = value

    half = lax.axis_index("ml") // (sources // HALVES)
    mine = pl.ds(pl.multiple_of(half * own, own), own)
    key = jnp.transpose(
        jnp.dot(read[channels:], hidden_ref[...], preferred_element_type=F32)
    ).astype(BF16)
    query = jnp.dot(read[:channels], hidden_ref[:, mine], preferred_element_type=F32).astype(BF16)
    side = side_ref[...]
    total = jnp.zeros((16, own), F32)
    for here in parts:
        pull = jnp.dot(key[here], query, preferred_element_type=F32) * (
            pull_ref[here, mine] * (1.0 / channels)
        )
        high = pull.astype(BF16)
        rest = (pull - high.astype(F32)).astype(BF16)
        total += jnp.dot(side[:, here], high, preferred_element_type=F32)
        total += jnp.dot(side[:, here], rest, preferred_element_type=F32)
    sums = total[0:4] + total[4:8] + total[8:12]
    force = sums[0:3] - pos_ref[0:3, mine] * sums[3:4]
    force_ref[...] = jnp.zeros_like(force_ref)
    for place, a in enumerate(exchange_order(own // share)):
        force_ref[place, 0:3, 0:share] = force[:, share * a : share * (a + 1)]


def pair_kernel(
    tiles_hbm_ref,
    own_ref,
    low_ref,
    high_ref,
    force_ref,
    rows_ref,
    value_ref,
    near_ref,
    side_ref,
    mine_ref,
    tiles_ref,
    tiles_sem,
):
    listed, tiles = tiles_ref.shape
    tiles_copy = pltpu.make_async_copy(tiles_hbm_ref, tiles_ref, tiles_sem)
    tiles_copy.start()
    for which, ref in enumerate((low_ref, own_ref, high_ref)):
        place = ref[...]
        pieces = split(place)
        norm = norm_of(place)
        right_rows(rows_ref, pieces, norm)
        charge = place[3:4]
        weighted = jnp.concatenate([place[0:3] * charge, charge], axis=0)
        for g, value in enumerate(split(weighted)):
            value_ref[4 * g : 4 * g + 4, :] = value
        value_ref[12:16, :] = jnp.zeros_like(place)
        for t in range(tiles):
            lanes = slice(TILE * t, TILE * (t + 1))
            near_ref[which * tiles + t] = rows_ref[:, lanes].astype(BF16)
            side_ref[which * tiles + t] = value_ref[:, lanes].astype(BF16)
    place = own_ref[...]
    is_place = lax.broadcasted_iota(jnp.int32, place.shape, 0) < 3
    left_rows(rows_ref, [jnp.where(is_place, piece, 0.0) for piece in split(place)], norm_of(place))
    for t in range(tiles):
        lanes = slice(TILE * t, TILE * (t + 1))
        mine_ref[lanes, :] = jnp.transpose(rows_ref[:, lanes]).astype(BF16)
    across = (((1,), (1,)), ((), ()))
    tiles_copy.wait()
    for t in range(tiles):
        lanes = slice(TILE * t, TILE * (t + 1))
        mine = mine_ref[lanes, :]
        total = jnp.zeros((TILE, 16), F32)
        for c in range(0, listed, 2):
            first, second = tiles_ref[c, t], tiles_ref[c + 1, t]
            squared = jnp.dot(
                mine,
                jnp.concatenate([near_ref[first], near_ref[second]], axis=1),
                preferred_element_type=F32,
            )
            inverse = lax.rsqrt(squared)
            total += lax.dot_general(
                (inverse * inverse * inverse).astype(BF16),
                jnp.concatenate([side_ref[first], side_ref[second]], axis=1),
                across,
                preferred_element_type=F32,
            )
        turned = jnp.transpose(total)
        sums = turned[0:4] + turned[4:8] + turned[8:12]
        place = own_ref[:, lanes]
        force_ref[:, lanes] = (place[0:3] * sums[3:4] - sums[0:3]) * (place[3:4] * COULOMB)


def vmem(count):
    return [pl.BlockSpec(memory_space=pltpu.VMEM)] * count


def on_device(
    mm_positions,
    mm_charge,
    mm_tiles,
    ml_feat,
    ml_positions,
    ml_neighbours,
    msg_weight,
    radial_weight,
    out_weight,
    read_weight,
):
    patches, share, channels = ml_feat.shape
    atom_count = mm_positions.shape[1]
    tile_count, listed = mm_tiles.shape
    members = lax.axis_size("ml")
    size = members * share
    own = size // HALVES
    neighbours = ml_neighbours.shape[1]
    basis_count = radial_weight.shape[1]
    limit = 48 * 1024 * 1024

    send, atoms, near_radial = pl.pallas_call(
        pack_kernel,
        out_shape=(
            jax.ShapeDtypeStruct((members, share + 16, channels), BF16),
            pltpu.VMEM((4, atom_count), F32),
            pltpu.VMEM(radial_weight.shape, F32),
        ),
        in_specs=vmem(6),
        out_specs=tuple(vmem(3)),
        scratch_shapes=[pltpu.VMEM((patches, 16, 128), F32)],
        cost_estimate=pl.CostEstimate(flops=1000, bytes_accessed=400000, transcendentals=0),
    )(
        ml_feat,
        ml_positions.transpose(1, 0, 2),
        ml_neighbours,
        mm_positions,
        mm_charge.reshape(1, atom_count),
        radial_weight,
    )
    recv = lax.all_to_all(
        send,
        "ml",
        split_axis=0,
        concat_axis=0,
        tiled=True,
        axis_index_groups=[exchange_order(members)],
    )

    devices = lax.axis_size(("dom", "ml"))
    forward = [(i, (i + 1) % devices) for i in range(devices)]
    backward = [(b, a) for a, b in forward]
    low = lax.ppermute(atoms, ("dom", "ml"), forward)
    high = lax.ppermute(atoms, ("dom", "ml"), backward)

    forces = pl.pallas_call(
        patch_kernel,
        out_shape=jax.ShapeDtypeStruct((own // share, 8, 128), F32),
        in_specs=vmem(5),
        out_specs=vmem(1)[0],
        scratch_shapes=[
            pltpu.VMEM((size, channels), BF16),
            pltpu.VMEM((channels, size), BF16),
            pltpu.VMEM((8, size), F32),
            pltpu.VMEM((32, size), F32),
            pltpu.VMEM((32, size), BF16),
            pltpu.VMEM((size, 32), BF16),
            pltpu.VMEM((16, size), BF16),
            pltpu.VMEM((neighbours, size), jnp.int32),
            pltpu.VMEM((neighbours, size), jnp.int32),
            pltpu.VMEM((-(-size // (8 * FIELDS)) * 8, size), jnp.int32),
            pltpu.VMEM((size, size), F32),
            pltpu.VMEM((basis_count, size, size), BF16),
            pltpu.VMEM((size, size), F32),
        ],
        compiler_params=pltpu.CompilerParams(vmem_limit_bytes=limit),
        cost_estimate=pl.CostEstimate(
            flops=5 * 10**9, bytes_accessed=1000000, transcendentals=10**6
        ),
    )(recv, msg_weight, near_radial, out_weight, read_weight)
    groups = [[h * patches + p for p in exchange_order(patches)] for h in range(HALVES)]
    returned = lax.all_to_all(
        forces, "ml", split_axis=0, concat_axis=0, tiled=True, axis_index_groups=groups
    )
    ml_force = returned[:, :3, :share]

    mm_force = pl.pallas_call(
        pair_kernel,
        out_shape=jax.ShapeDtypeStruct((3, atom_count), F32),
        in_specs=[pl.BlockSpec(memory_space=pl.ANY)] + vmem(3),
        out_specs=vmem(1)[0],
        scratch_shapes=[
            pltpu.VMEM((32, atom_count), F32),
            pltpu.VMEM((16, atom_count), F32),
            pltpu.VMEM((3 * tile_count, 32, TILE), BF16),
            pltpu.VMEM((3 * tile_count, 16, TILE), BF16),
            pltpu.VMEM((atom_count, 32), BF16),
            pltpu.SMEM((listed, tile_count), jnp.int32),
            pltpu.SemaphoreType.DMA,
        ],
        compiler_params=pltpu.CompilerParams(vmem_limit_bytes=limit),
        cost_estimate=pl.CostEstimate(
            flops=4 * 10**9, bytes_accessed=200000, transcendentals=10**6
        ),
    )(mm_tiles.T, atoms, low, high)
    return (mm_force, ml_force)


def solution(mesh):
    in_specs = (
        P(None, ("dom", "ml")),
        P(("dom", "ml")),
        P(("dom", "ml"), None),
        P("dom", "ml", None),
        P("dom", None, "ml"),
        P("dom", None, "ml"),
        P(),
        P(),
        P(),
        P(),
    )
    out_specs = (P(None, ("dom", "ml")), P("dom", None, "ml"))
    return jax.shard_map(
        on_device, mesh=mesh, in_specs=in_specs, out_specs=out_specs, check_vma=False
    )
```

```python
import math

import jax
import jax.numpy as jnp
from jax import lax
from jax.experimental import pallas as pl
from jax.experimental.pallas import tpu as pltpu
from jax.sharding import PartitionSpec as P

TILE = 128
RADIUS = 6.0
SOFTEN = 1.0
COULOMB = 0.5
HALVES = 2
FIELDS = 5
BITS = 6


FIRST = {16: 11, 8: 2}
EIGHT = (2, 3, 6, 0, 7, 4, 5, 1)


def exchange_order(count):
    if count == len(EIGHT):
        return list(EIGHT)
    first = FIRST.get(count, count - 1)
    return [first] + [member for member in range(count)[::-1] if member != first]


COSINE = (
    0.9999999991255941,
    -0.23370050635000697,
    0.019968606683524803,
    -0.0008935362638784474,
    2.3601070666008123e-05,
)

F32 = jnp.float32
BF16 = jnp.bfloat16


def split(value):
    high = value.astype(BF16).astype(F32)
    rest = value - high
    middle = rest.astype(BF16).astype(F32)
    return high, middle, rest - middle


LEFT = (0, 0, 1, 1, 0, 2)
RIGHT = (0, 1, 0, 1, 2, 0)


def left_rows(rows_ref, pieces, norm):
    for g, which in enumerate(LEFT):
        rows_ref[4 * g : 4 * g + 4, :] = pieces[which]
    for g, value in enumerate(split(norm + SOFTEN)):
        rows_ref[24 + g : 25 + g, :] = value
    rows_ref[27:30, :] = jnp.ones((3, norm.shape[1]), F32)
    rows_ref[30:32, :] = jnp.zeros((2, norm.shape[1]), F32)


def right_rows(rows_ref, pieces, norm):
    for g, which in enumerate(RIGHT):
        rows_ref[4 * g : 4 * g + 4, :] = pieces[which] * -2.0
    rows_ref[24:27, :] = jnp.ones((3, norm.shape[1]), F32)
    for g, value in enumerate(split(norm)):
        rows_ref[27 + g : 28 + g, :] = value
    rows_ref[30:32, :] = jnp.zeros((2, norm.shape[1]), F32)


def norm_of(place):
    return place[0:1] * place[0:1] + place[1:2] * place[1:2] + place[2:3] * place[2:3]


def pack_kernel(
    feat_ref,
    pos_ref,
    nb_ref,
    mm_pos_ref,
    mm_charge_ref,
    radial_ref,
    send_ref,
    atoms_ref,
    near_radial_ref,
    geo_ref,
):
    patches, atoms, _ = feat_ref.shape
    members = send_ref.shape[0]
    holder = exchange_order(patches)
    geo_ref[...] = jnp.zeros_like(geo_ref)
    high, middle, low = split(pos_ref[...])
    for p in range(patches):
        numbers = (nb_ref[p] - 256).astype(F32)
        geo_ref[p, 0:16, 0:32] = numbers[0:16]
        geo_ref[p, 0:16, 32:64] = numbers[16:32]
        for axis in range(3):
            geo_ref[p, axis : axis + 1, 64:96] = high[axis, p : p + 1]
            geo_ref[p, axis : axis + 1, 96:128] = middle[axis, p : p + 1]
            geo_ref[p, axis + 8 : axis + 9, 64:96] = low[axis, p : p + 1]
        block = geo_ref[p].astype(BF16)
        for place, member in enumerate(exchange_order(members)):
            if member % patches == holder[p]:
                send_ref[place, 0:atoms, :] = feat_ref[p]
                send_ref[place, atoms : atoms + 16, :] = block
    atoms_ref[0:3, :] = mm_pos_ref[...]
    atoms_ref[3:4, :] = mm_charge_ref[...]
    near_radial_ref[...] = radial_ref[...]


def patch_kernel(
    recv_ref,
    msg_ref,
    radial_ref,
    out_w_ref,
    read_ref,
    force_ref,
    plain_ref,
    hidden_ref,
    pos_ref,
    rows_ref,
    near_ref,
    mine_ref,
    side_ref,
    low_ref,
    unit_ref,
    count_ref,
    square_ref,
    basis_ref,
    pull_ref,
):
    sources = recv_ref.shape[0]
    share = recv_ref.shape[1] - 16
    size = sources * share
    own = size // HALVES
    neighbours = low_ref.shape[0]
    basis_count = radial_ref.shape[1]
    layers = msg_ref.shape[0]
    channels = recv_ref.shape[2]
    tiles = size // 128

    for place, m in enumerate(exchange_order(sources)):
        plain_ref[share * m : share * (m + 1), :] = recv_ref[place, 0:share, :]
        geo = recv_ref[place, share : share + 16, :].astype(F32)
        lanes = slice(share * m, share * (m + 1))
        pos_ref[:, lanes] = (geo[0:8, 64:96] + geo[0:8, 96:128]) + geo[8:16, 64:96]
        low_ref[0:16, lanes] = geo[:, 0:32].astype(jnp.int32) + 256
        low_ref[16:32, lanes] = geo[:, 32:64].astype(jnp.int32) + 256
    hidden_ref[...] = jnp.transpose(plain_ref[...])
    msg = [jnp.transpose(msg_ref[layer]) for layer in range(layers)]
    out_w = [jnp.transpose(out_w_ref[layer]) for layer in range(layers)]
    read = jnp.transpose(read_ref[...])

    def mix(layer):
        return jnp.dot(msg[layer], hidden_ref[...], preferred_element_type=F32).astype(BF16)

    mixed = mix(0)

    place = pos_ref[0:4, :]
    pieces = split(place)
    norm = norm_of(place)
    right_rows(rows_ref, pieces, norm)
    near_ref[...] = rows_ref[...].astype(BF16)
    left_rows(rows_ref, pieces, norm)
    for b in range(tiles):
        at = slice(128 * b, 128 * (b + 1))
        mine_ref[at, :] = jnp.transpose(rows_ref[:, at]).astype(BF16)
    for g, value in enumerate(pieces):
        rows_ref[4 * g : 4 * g + 4, :] = value
    rows_ref[3:4, :] = jnp.ones((1, size), F32)
    rows_ref[12:16, :] = jnp.zeros((4, size), F32)
    side_ref[...] = rows_ref[0:16, :].astype(BF16)
    square_ref[...] = jnp.dot(mine_ref[...], near_ref[...], preferred_element_type=F32)

    index = low_ref[...]
    depth = count_ref.shape[0]
    field = jnp.zeros_like(index)
    for f in range(1, FIELDS):
        field += (index >= depth * f).astype(jnp.int32)
    low_ref[...] = index - field * depth
    unit_ref[...] = jnp.int32(1) << (field * BITS)
    rows = lax.broadcasted_iota(jnp.int32, (depth, 128), 0)

    def count(b):
        lanes = slice(128 * b, 128 * (b + 1))
        total = jnp.zeros((depth, 128), jnp.int32)
        for k in range(neighbours):
            total += jnp.where(rows == low_ref[k : k + 1, lanes], unit_ref[k : k + 1, lanes], 0)
        count_ref[:, lanes] = total

    step = 32
    limit = RADIUS * RADIUS
    per_basis = 4.0 * RADIUS / basis_count / math.log(2.0)
    series = [value / limit ** (k + 1) for k, value in enumerate(COSINE)]

    def pairs(lanes):
        for s in range(size // step):
            here = slice(step * s, step * (s + 1))
            found = []
            for group in range(0, step, 8):
                f, first = divmod(step * s + group, depth)
                packed = count_ref[first : first + 8, lanes]
                found.append((packed >> (BITS * f)) & ((1 << BITS) - 1))
            times = jnp.concatenate(found, axis=0).astype(F32)
            near = jnp.minimum(square_ref[here, lanes], limit)
            root = series[-1]
            for value in series[-2::-1]:
                root = root * near + value
            root = (limit - near) * root
            envelope = root * root * times
            pull_ref[here, lanes] = envelope
            growth = jnp.exp2(near * lax.rsqrt(near) * per_basis)
            basis = jnp.exp2(near * (-2.0 / math.log(2.0))) * envelope
            for n in range(basis_count):
                basis_ref[n, here, lanes] = basis.astype(BF16)
                if n + 1 < basis_count:
                    basis = basis * growth

    number = lax.broadcasted_iota(jnp.int32, (basis_count, channels), 0).astype(F32)
    center = number * (RADIUS / basis_count)
    scale = jnp.exp(center * center * -2.0) * (1.0 / math.sqrt(neighbours))
    radial = [jnp.transpose(radial_ref[layer] * scale) for layer in range(layers)]

    def advance(layer, lanes, mixed):
        message = 0.0
        for n in range(basis_count):
            message += radial[layer][:, n : n + 1] * jnp.dot(
                mixed, basis_ref[n, :, lanes], preferred_element_type=F32
            )
        active = jax.nn.silu(message).astype(BF16)
        change = jnp.dot(out_w[layer], active, preferred_element_type=F32)
        return (hidden_ref[:, lanes].astype(F32) + change).astype(BF16)

    parts = [slice(own * part, own * (part + 1)) for part in range(HALVES)]
    for part, lanes in enumerate(parts):
        for b in range(tiles // HALVES):
            count(tiles // HALVES * part + b)
        pairs(lanes)
    for layer in range(layers):
        if layer > 0:
            mixed = mix(layer)
        later = [advance(layer, lanes, mixed) for lanes in parts]
        for lanes, value in zip(parts, later):
            hidden_ref[:, lanes] = value

    half = lax.axis_index("ml") // (sources // HALVES)
    mine = pl.ds(pl.multiple_of(half * own, own), own)
    key = jnp.transpose(
        jnp.dot(read[channels:], hidden_ref[...], preferred_element_type=F32)
    ).astype(BF16)
    query = jnp.dot(read[:channels], hidden_ref[:, mine], preferred_element_type=F32).astype(BF16)
    side = side_ref[...]
    total = jnp.zeros((16, own), F32)
    for here in parts:
        pull = jnp.dot(key[here], query, preferred_element_type=F32) * (
            pull_ref[here, mine] * (1.0 / channels)
        )
        high = pull.astype(BF16)
        rest = (pull - high.astype(F32)).astype(BF16)
        total += jnp.dot(side[:, here], high, preferred_element_type=F32)
        total += jnp.dot(side[:, here], rest, preferred_element_type=F32)
    sums = total[0:4] + total[4:8] + total[8:12]
    force = sums[0:3] - pos_ref[0:3, mine] * sums[3:4]
    force_ref[...] = jnp.zeros_like(force_ref)
    for place, a in enumerate(exchange_order(own // share)):
        force_ref[place, 0:3, 0:share] = force[:, share * a : share * (a + 1)]


def pair_kernel(
    tiles_hbm_ref,
    own_ref,
    low_ref,
    high_ref,
    force_ref,
    rows_ref,
    value_ref,
    near_ref,
    side_ref,
    mine_ref,
    tiles_ref,
    tiles_sem,
):
    listed, tiles = tiles_ref.shape
    tiles_copy = pltpu.make_async_copy(tiles_hbm_ref, tiles_ref, tiles_sem)
    tiles_copy.start()
    for which, ref in enumerate((low_ref, own_ref, high_ref)):
        place = ref[...]
        pieces = split(place)
        norm = norm_of(place)
        right_rows(rows_ref, pieces, norm)
        charge = place[3:4]
        weighted = jnp.concatenate([place[0:3] * charge, charge], axis=0)
        for g, value in enumerate(split(weighted)):
            value_ref[4 * g : 4 * g + 4, :] = value
        value_ref[12:16, :] = jnp.zeros_like(place)
        for t in range(tiles):
            lanes = slice(TILE * t, TILE * (t + 1))
            near_ref[which * tiles + t] = rows_ref[:, lanes].astype(BF16)
            side_ref[which * tiles + t] = value_ref[:, lanes].astype(BF16)
    place = own_ref[...]
    is_place = lax.broadcasted_iota(jnp.int32, place.shape, 0) < 3
    left_rows(rows_ref, [jnp.where(is_place, piece, 0.0) for piece in split(place)], norm_of(place))
    for t in range(tiles):
        lanes = slice(TILE * t, TILE * (t + 1))
        mine_ref[lanes, :] = jnp.transpose(rows_ref[:, lanes]).astype(BF16)
    across = (((1,), (1,)), ((), ()))
    tiles_copy.wait()
    for t in range(tiles):
        lanes = slice(TILE * t, TILE * (t + 1))
        mine = mine_ref[lanes, :]
        total = jnp.zeros((TILE, 16), F32)
        for c in range(0, listed, 2):
            first, second = tiles_ref[c, t], tiles_ref[c + 1, t]
            squared = jnp.dot(
                mine,
                jnp.concatenate([near_ref[first], near_ref[second]], axis=1),
                preferred_element_type=F32,
            )
            inverse = lax.rsqrt(squared)
            total += lax.dot_general(
                (inverse * inverse * inverse).astype(BF16),
                jnp.concatenate([side_ref[first], side_ref[second]], axis=1),
                across,
                preferred_element_type=F32,
            )
        turned = jnp.transpose(total)
        sums = turned[0:4] + turned[4:8] + turned[8:12]
        place = own_ref[:, lanes]
        force_ref[:, lanes] = (place[0:3] * sums[3:4] - sums[0:3]) * (place[3:4] * COULOMB)


def vmem(count):
    return [pl.BlockSpec(memory_space=pltpu.VMEM)] * count


def on_device(
    mm_positions,
    mm_charge,
    mm_tiles,
    ml_feat,
    ml_positions,
    ml_neighbours,
    msg_weight,
    radial_weight,
    out_weight,
    read_weight,
):
    patches, share, channels = ml_feat.shape
    atom_count = mm_positions.shape[1]
    tile_count, listed = mm_tiles.shape
    members = lax.axis_size("ml")
    size = members * share
    own = size // HALVES
    neighbours = ml_neighbours.shape[1]
    basis_count = radial_weight.shape[1]
    limit = 48 * 1024 * 1024

    send, atoms, near_radial = pl.pallas_call(
        pack_kernel,
        out_shape=(
            jax.ShapeDtypeStruct((members, share + 16, channels), BF16),
            pltpu.VMEM((4, atom_count), F32),
            pltpu.VMEM(radial_weight.shape, F32),
        ),
        in_specs=vmem(6),
        out_specs=tuple(vmem(3)),
        scratch_shapes=[pltpu.VMEM((patches, 16, 128), F32)],
        cost_estimate=pl.CostEstimate(flops=1000, bytes_accessed=400000, transcendentals=0),
    )(
        ml_feat,
        ml_positions.transpose(1, 0, 2),
        ml_neighbours,
        mm_positions,
        mm_charge.reshape(1, atom_count),
        radial_weight,
    )
    recv = lax.all_to_all(
        send,
        "ml",
        split_axis=0,
        concat_axis=0,
        tiled=True,
        axis_index_groups=[exchange_order(members)],
    )

    devices = lax.axis_size(("dom", "ml"))
    forward = [(i, (i + 1) % devices) for i in range(devices)]
    backward = [(b, a) for a, b in forward]
    low = lax.ppermute(atoms, ("dom", "ml"), forward)
    high = lax.ppermute(atoms, ("dom", "ml"), backward)

    forces = pl.pallas_call(
        patch_kernel,
        out_shape=jax.ShapeDtypeStruct((own // share, 8, 128), F32),
        in_specs=vmem(5),
        out_specs=vmem(1)[0],
        scratch_shapes=[
            pltpu.VMEM((size, channels), BF16),
            pltpu.VMEM((channels, size), BF16),
            pltpu.VMEM((8, size), F32),
            pltpu.VMEM((32, size), F32),
            pltpu.VMEM((32, size), BF16),
            pltpu.VMEM((size, 32), BF16),
            pltpu.VMEM((16, size), BF16),
            pltpu.VMEM((neighbours, size), jnp.int32),
            pltpu.VMEM((neighbours, size), jnp.int32),
            pltpu.VMEM((-(-size // (8 * FIELDS)) * 8, size), jnp.int32),
            pltpu.VMEM((size, size), F32),
            pltpu.VMEM((basis_count, size, size), BF16),
            pltpu.VMEM((size, size), F32),
        ],
        compiler_params=pltpu.CompilerParams(vmem_limit_bytes=limit),
        cost_estimate=pl.CostEstimate(
            flops=5 * 10**9, bytes_accessed=1000000, transcendentals=10**6
        ),
    )(recv, msg_weight, near_radial, out_weight, read_weight)
    groups = [[h * patches + p for p in exchange_order(patches)] for h in range(HALVES)]
    returned = lax.all_to_all(
        forces, "ml", split_axis=0, concat_axis=0, tiled=True, axis_index_groups=groups
    )
    ml_force = returned[:, :3, :share]

    mm_force = pl.pallas_call(
        pair_kernel,
        out_shape=jax.ShapeDtypeStruct((3, atom_count), F32),
        in_specs=[pl.BlockSpec(memory_space=pl.ANY)] + vmem(3),
        out_specs=vmem(1)[0],
        scratch_shapes=[
            pltpu.VMEM((32, atom_count), F32),
            pltpu.VMEM((16, atom_count), F32),
            pltpu.VMEM((3 * tile_count, 32, TILE), BF16),
            pltpu.VMEM((3 * tile_count, 16, TILE), BF16),
            pltpu.VMEM((atom_count, 32), BF16),
            pltpu.SMEM((listed, tile_count), jnp.int32),
            pltpu.SemaphoreType.DMA,
        ],
        compiler_params=pltpu.CompilerParams(vmem_limit_bytes=limit),
        cost_estimate=pl.CostEstimate(
            flops=4 * 10**9, bytes_accessed=200000, transcendentals=10**6
        ),
    )(mm_tiles.T, atoms, low, high)
    return (mm_force, ml_force)


def solution(mesh):
    in_specs = (
        P(None, ("dom", "ml")),
        P(("dom", "ml")),
        P(("dom", "ml"), None),
        P("dom", "ml", None),
        P("dom", None, "ml"),
        P("dom", None, "ml"),
        P(),
        P(),
        P(),
        P(),
    )
    out_specs = (P(None, ("dom", "ml")), P("dom", None, "ml"))
    return jax.shard_map(
        on_device, mesh=mesh, in_specs=in_specs, out_specs=out_specs, check_vma=False
    )
```
